32 devices in a mesh: group: 2 (over x), seq: 16 (over z, y, core).
Axes of the slice: x: 2, y: 2, z: 4, core: 2. Of those that a mesh axis runs over, the one named last changes fastest.
Arguments:
- tokens: bfloat16 [256, 8192], P('group', 'seq'), parts along dimension 0, may hold values from -1700 to 1700
- gain: bfloat16 [8192], P('seq'), may hold values from 0.099609375 to 1.8984375
- w_query: bfloat16 [8192, 8192], P('seq'), may hold values from -0.0625 to 0.0625
- w_key: bfloat16 [1024, 8192], P('seq'), may hold values from -0.375 to 0.375
- w_value: bfloat16 [1024, 8192], P('seq'), may hold values from -0.0625 to 0.0625
- w_out: bfloat16 [8192, 8192], P('seq'), may hold values from -0.09375 to 0.09375
- prefix_cache: bfloat16 [2, 8192, 1024], P(None, ('group', 'seq')), parts along dimension 1, may hold values from -2700 to 2700
Outputs:
- mixed: bfloat16 [256, 8192], P('group', 'seq'), parts along dimension 0
The draws below stay inside these ranges and needn't reach their ends.
There are 2 independent parts, one for each index of `group`. The reference program is written for one: setup_inputs(seed, part) draws one part's arguments, and reference() takes and returns one part's arrays. A program takes and returns all parts, laid end to end along the dimension named above; an argument that names none is the same for every part. Nothing has to cross between parts.
All inputs are finite; a program needn't handle non-finite values.
Results may differ from the reference program's by a relative error of at most 0.014.
The reference program's roundings to bfloat16 on the way (of `normed`, `query`, `key_own`, `value_own` and `attention`) count: a program that leaves them out, or rounds other values in their place, can miss the bound.
Values may be sent and summed in bfloat16 or wider, within the bound.
No kernel may reach another device: no remote copies, remote signals or barrier semaphores. Data moves between devices by JAX's collectives and lax.ppermute only.
A program may use at most 64 MiB of HBM per device.

```python
import math
import jax
import jax.numpy as jnp
from jax import lax

D = 8192
H = 64
KV = 8
DH = 128
R = 128
PREFIX = 4096


def draw_tokens(key, part):
    key_rows, key_cols, key_base = jax.random.split(key, 3)
    row_top = 10.0
    ramp_top = 10.0
    base = jnp.clip(jax.random.normal(key_base, (R, D)), -4.0, 4.0)
    row_scale = jnp.exp(jax.random.uniform(key_rows, (R, 1), minval=0.0, maxval=jnp.log(row_top)))
    ramp = jnp.exp(jnp.log(ramp_top) * jnp.arange(D, dtype=jnp.float32) / D)
    col_scale = ramp * jnp.exp(jax.random.uniform(key_cols, (D,), minval=-0.7, maxval=0.7))
    return (base * row_scale * col_scale[None, :]).astype(jnp.bfloat16)


def draw_prefix_cache(key, part):
    key_keys, key_values = jax.random.split(key, 2)
    cached_keys = 3.0 * jnp.clip(jax.random.normal(key_keys, (PREFIX, KV * DH)), -5.0, 5.0)
    cached_values = jnp.clip(jax.random.normal(key_values, (PREFIX, KV * DH)), -5.0, 5.0)
    return jnp.stack([cached_keys, cached_values]).astype(jnp.bfloat16)


def spiked(values, key, source, target, shards_of, factor):
    owner, partner = [(jnp.arange(values.shape[dim]) // (values.shape[dim] // shards_of)).reshape([-1 if axis == dim else 1 for axis in range(values.ndim)]) for dim in (source, target)]
    chosen = jax.random.permutation(key, shards_of)[partner]
    strong = (owner == chosen) | (owner == (partner + shards_of // 2) % shards_of)
    return jnp.where(strong, factor * values, values)


def level_of(rng, extent, shards, smallest, largest):
    level, own = 1.0, jax.random.fold_in(rng, 6)
    for dim, shards_of in shards:
        draws = jnp.exp(jax.random.uniform(jax.random.fold_in(own, dim), (shards_of,), jnp.float32, smallest / len(shards), largest / len(shards)))
        level = level * jnp.repeat(draws, extent[dim] // shards_of).reshape([-1 if axis == dim else 1 for axis in range(len(extent))])
    return level


def centred(rng, extent, deviation, bound, pieces=(), kind=jnp.bfloat16):
    level = level_of(rng, extent, pieces, -0.22, 0.18) if pieces else 1.0
    result = jax.random.normal(rng, extent, jnp.float32) * deviation * level
    return jnp.minimum(jnp.maximum(result, -bound), bound).astype(kind)


def bell_draw_with(rng, shape, scale, bound, shards, heavy, kind=jnp.bfloat16):
    values = scale * jax.random.normal(rng, shape, jnp.float32)
    if shards:
        values = values * level_of(rng, shape, shards, -0.22, 0.18)
    return jnp.clip(spiked(values, jax.random.fold_in(rng, 3), *heavy), -bound, bound).astype(kind)


def setup_inputs(seed: int = 0, part: int = 0) -> dict:
    splits = jax.random.split(jax.random.key(seed), 8)
    own_keys = jax.random.split(jax.random.fold_in(splits[7], part), 8)
    return {
        "tokens": draw_tokens(jax.random.fold_in(jax.random.fold_in(splits[7], part), 71), part),
        "gain": jnp.clip(1.0 + 0.18 * jax.random.normal(splits[1], (D,), jnp.float32), 0.099609375, 1.8984375).astype(jnp.bfloat16),
        "w_query": centred(splits[2], (H * DH, D), D ** -0.5, 0.0625, ((0, 16),)),
        "w_key": centred(splits[3], (KV * DH, D), (D // 36) ** -0.5, 0.375, ((0, 16),)),
        "w_value": centred(splits[4], (KV * DH, D), D ** -0.5, 0.0625, ((0, 16),)),
        "w_out": bell_draw_with(splits[5], (H * DH, D), (H * DH) ** -0.5, 0.09375, ((0, 16),), (0, 1, 16, 2.0)),
        "prefix_cache": draw_prefix_cache(jax.random.fold_in(jax.random.fold_in(splits[7], part), 71), part),
    }


def normalize(tokens, gain):
    wide_tokens = tokens.astype(jnp.float32)
    inverse = lax.rsqrt(lax.optimization_barrier(jnp.mean(wide_tokens * wide_tokens, axis=1, keepdims=True)) + 1e-05)
    return (wide_tokens * inverse * gain.astype(jnp.float32)).astype(jnp.bfloat16)

def reference(tokens, gain, w_query, w_key, w_value, w_out, prefix_cache):
    contract_dims = (((1,), (1,)), ((), ()))
    normed = normalize(tokens, gain)
    query = lax.dot_general(normed, w_query, contract_dims, preferred_element_type=jnp.float32).astype(jnp.bfloat16)
    key_own = lax.dot_general(normed, w_key, contract_dims, preferred_element_type=jnp.float32).astype(jnp.bfloat16)
    value_own = lax.dot_general(normed, w_value, contract_dims, preferred_element_type=jnp.float32).astype(jnp.bfloat16)
    row_count = tokens.shape[0]
    group_size = H // KV
    score_scale = 1.0 / math.sqrt(DH)
    query_heads = query.reshape(row_count, KV, group_size, DH).astype(jnp.float32)
    key_heads = key_own.reshape(row_count, KV, DH).astype(jnp.float32)
    own_scores = jnp.einsum('rgjd,rgd->rgj', query_heads, key_heads) * score_scale
    value_heads = value_own.reshape(row_count, KV, DH)
    results = []
    for head_group in range(KV):
        query_group = query.reshape(row_count, KV, group_size * DH)[:, head_group].reshape(row_count * group_size, DH)
        keys_group = prefix_cache[0][:, head_group * DH:(head_group + 1) * DH]
        values_group = prefix_cache[1][:, head_group * DH:(head_group + 1) * DH]
        scores = lax.dot_general(query_group, keys_group, contract_dims, preferred_element_type=jnp.float32) * score_scale
        own_group = own_scores[:, head_group].reshape(row_count * group_size)
        row_max = jnp.maximum(lax.optimization_barrier(jnp.max(scores, axis=1)), own_group)
        weights = jnp.exp(scores - row_max[:, None])
        own_weight = jnp.exp(own_group - row_max)
        denominator = lax.optimization_barrier(jnp.sum(weights, axis=1)) + own_weight
        numerator = jnp.dot(weights.astype(jnp.bfloat16), values_group, preferred_element_type=jnp.float32)
        own_values = jnp.repeat(value_heads[:, head_group], group_size, axis=0).astype(jnp.float32)
        rounded = lax.optimization_barrier(own_weight.astype(jnp.bfloat16)).astype(jnp.float32)
        numerator = numerator + rounded[:, None] * own_values
        results.append((numerator / denominator[:, None]).astype(jnp.bfloat16).reshape(row_count, group_size * DH))
    attention = jnp.concatenate(results, axis=1)
    return jnp.dot(attention, w_out, preferred_element_type=jnp.float32).astype(jnp.bfloat16)
```

```python
import functools
import math

import jax
import jax.numpy as jnp
from jax import lax
from jax.experimental import pallas as pl
from jax.experimental.pallas import tpu as pltpu
from jax.sharding import PartitionSpec as P

H = 64
KV = 8
DH = 128
EPS = 1e-05
PAD = 16
MIB = 1 << 20
TRANS_B = (((1,), (1,)), ((), ()))


def vmem_specs(count):
    return [pl.BlockSpec(memory_space=pltpu.VMEM)] * count


def project_kernel(count, rows, owner_ref, *refs):
    blocks, (w_query, w_key, w_value, query_ref, own_ref) = refs[:count], refs[count:]
    width = blocks[0].shape[1]
    total = jnp.zeros((rows, 1), jnp.float32)
    for block in blocks:
        wide = block[:rows, :].astype(jnp.float32)
        total += jnp.sum(wide * wide, axis=1, keepdims=True)
    inverse = lax.rsqrt(total / (width * count) + EPS)
    query = jnp.zeros(query_ref.shape, jnp.float32)
    key = jnp.zeros((rows, w_key.shape[0]), jnp.float32)
    value = jnp.zeros((rows, w_key.shape[0]), jnp.float32)
    for number, block in enumerate(blocks):
        gain = block[rows : rows + PAD, :].astype(jnp.float32)[0:1, :]
        wide = block[:rows, :].astype(jnp.float32)
        normed = (wide * inverse * gain).astype(jnp.bfloat16)
        columns = pl.ds(pl.multiple_of(owner_ref[number] * width, width), width)
        query += lax.dot_general(normed, w_query[:, columns], TRANS_B, preferred_element_type=jnp.float32)
        key += lax.dot_general(normed, w_key[:, columns], TRANS_B, preferred_element_type=jnp.float32)
        value += lax.dot_general(normed, w_value[:, columns], TRANS_B, preferred_element_type=jnp.float32)
    query_ref[...] = query.astype(jnp.bfloat16)
    own_ref[...] = jnp.concatenate([key, value], axis=1).astype(jnp.bfloat16)


def project(owners, blocks, w_query, w_key, w_value, rows):
    count = len(blocks)
    return pl.pallas_call(
        functools.partial(project_kernel, count, rows),
        out_shape=(
            jax.ShapeDtypeStruct((rows, w_query.shape[0]), jnp.bfloat16),
            jax.ShapeDtypeStruct((rows, 2 * w_key.shape[0]), jnp.bfloat16),
        ),
        in_specs=[pl.BlockSpec(memory_space=pltpu.SMEM)] + vmem_specs(count + 3),
        out_specs=tuple(vmem_specs(2)),
        compiler_params=pltpu.CompilerParams(vmem_limit_bytes=48 * MIB),
        name="project",
    )(owners, *blocks, w_query, w_key, w_value)


def attend_kernel(count, heads, *refs):
    caches, (query_ref, own_key, own_value, out_ref, query_all, scores) = refs[:count], refs[count:]
    rows = query_ref.shape[0]
    scale = 1.0 / math.sqrt(DH)
    for head in range(heads):
        query_all[head * rows : (head + 1) * rows, :] = query_ref[:, head * DH : (head + 1) * DH]
    query = query_all[...]
    keys_own = jnp.concatenate([own_key[...].astype(jnp.float32)] * heads, axis=0)
    values_own = jnp.concatenate([own_value[...].astype(jnp.float32)] * heads, axis=0)
    own = jnp.sum(query.astype(jnp.float32) * keys_own, axis=1, keepdims=True) * scale
    step = caches[0].shape[1]
    best = None
    for number, cache in enumerate(caches):
        part = lax.dot_general(query, cache[0], TRANS_B, preferred_element_type=jnp.float32)
        scores[:, number * step : (number + 1) * step] = part
        for lane in range(0, step, 128):
            piece = part[:, lane : lane + 128]
            best = piece if best is None else jnp.maximum(best, piece)
    top = jnp.maximum(jnp.max(best, axis=1, keepdims=True) * scale, own)
    total = jnp.zeros((heads * rows, 128), jnp.float32)
    numerator = jnp.zeros((heads * rows, DH), jnp.float32)
    for number, cache in enumerate(caches):
        weights = jnp.exp(scores[:, number * step : (number + 1) * step] * scale - top)
        for lane in range(0, step, 128):
            total += weights[:, lane : lane + 128]
        numerator += jnp.dot(weights.astype(jnp.bfloat16), cache[1], preferred_element_type=jnp.float32)
    own_weight = jnp.exp(own - top)
    denominator = jnp.sum(total, axis=1, keepdims=True) + own_weight
    rounded = own_weight.astype(jnp.bfloat16).astype(jnp.float32)
    result = ((numerator + rounded * values_own) / denominator).astype(jnp.bfloat16)
    for head in range(heads):
        out_ref[:, head * DH : (head + 1) * DH] = result[head * rows : (head + 1) * rows, :]


def attend(caches, query, own_key, own_value):
    count, rows = len(caches), query.shape[0]
    heads = query.shape[1] // DH
    positions = count * caches[0].shape[1]
    return pl.pallas_call(
        functools.partial(attend_kernel, count, heads),
        out_shape=jax.ShapeDtypeStruct(query.shape, jnp.bfloat16),
        in_specs=vmem_specs(count + 3),
        out_specs=pl.BlockSpec(memory_space=pltpu.VMEM),
        scratch_shapes=[
            pltpu.VMEM((heads * rows, DH), jnp.bfloat16),
            pltpu.VMEM((heads * rows, positions), jnp.float32),
        ],
        compiler_params=pltpu.CompilerParams(vmem_limit_bytes=48 * MIB),
        name="attend",
    )(*caches, query, own_key, own_value)


def body(tokens, gain, w_query, w_key, w_value, w_out, prefix_cache, size):
    chips = size // 2
    outer = chips // 2
    cycle = [2 * a for a in range(outer)] + [2 * a + 1 for a in reversed(range(outer))]
    place_of = {chip: place for place, chip in enumerate(cycle)}
    places = jnp.array([place_of[chip] for chip in range(chips)], jnp.int32)
    cycle_array = jnp.array(cycle, jnp.int32)
    device = lax.axis_index("seq")
    chip, core = device // 2, device % 2
    place = places[chip]

    def around(value, step):
        pairs = [
            (2 * cycle[p] + k, 2 * cycle[(p + step) % chips] + k) for p in range(chips) for k in (0, 1)
        ]
        return lax.ppermute(value, "seq", pairs)

    def swap(value, bit):
        return lax.ppermute(value, "seq", [(i, i ^ bit) for i in range(size)])

    rows = tokens.shape[0]
    width = tokens.shape[1]

    positions = prefix_cache.shape[1]
    heads_here = jnp.repeat(prefix_cache.reshape(2, positions, KV, DH), chips // KV, axis=2) if chips > KV else prefix_cache.reshape(2, positions, KV, DH)
    by_chip = heads_here.reshape(2, positions, outer, 2, DH)
    inner = chip % 2
    to_keep = lax.dynamic_index_in_dim(by_chip, inner, 3, keepdims=False)
    to_send = lax.dynamic_index_in_dim(by_chip, 1 - inner, 3, keepdims=False)
    from_side = swap(to_send, 2)
    caches = []
    for step in range(outer):
        target = (chip // 2) ^ step
        for source in (to_keep, from_side):
            part = lax.dynamic_index_in_dim(source, target, 2, keepdims=False)
            part = swap(part, 4 * step) if step else part
            caches += [part, swap(part, 1)]

    block = jnp.concatenate([tokens, jnp.broadcast_to(gain[None, :], (PAD, width))], axis=0)
    blocks, owners = [], []

    def take(value, offset):
        owner = cycle_array[(place + offset) % chips]
        blocks.extend([value, swap(value, 1)])
        owners.extend([2 * owner + core, 2 * owner + 1 - core])

    take(block, 0)
    right = left = block
    for step in range(1, chips // 2 + 1):
        right = around(right, 1)
        take(right, chips - step)
        if step < chips // 2:
            left = around(left, -1)
            take(left, step)
    owners = jnp.stack(owners).astype(jnp.int32)
    query, own = project(owners, blocks, w_query, w_key, w_value, rows)

    local_heads = H // size
    sharers = size // KV
    half = own.shape[1] // 2
    own_parts = [own] if sharers == 1 else None
    if sharers == 2:
        other = swap(own, 1)
        first = jnp.where(core == 0, own, other)
        second = jnp.where(core == 0, other, own)
        own_parts = [first, second]
    elif own_parts is None:
        gathered = lax.all_gather(own, "seq", axis=0, axis_index_groups=[list(range(g * sharers, (g + 1) * sharers)) for g in range(KV)])
        own_parts = [gathered[i] for i in range(sharers)]
    own_key = jnp.concatenate([part[:, :half] for part in own_parts], axis=1)
    own_value = jnp.concatenate([part[:, half:] for part in own_parts], axis=1)
    attention = attend(caches, query, own_key, own_value)

    features = w_out.shape[1] // size
    partial = jnp.dot(attention, w_out, preferred_element_type=jnp.float32)
    partial = partial.astype(jnp.bfloat16).reshape(rows, chips, 2, features)
    mine = lax.dynamic_index_in_dim(partial, core, 2, keepdims=False)
    others = lax.dynamic_index_in_dim(partial, 1 - core, 2, keepdims=False)
    summed = mine.astype(jnp.float32) + swap(others, 1).astype(jnp.float32)

    def for_place(offset):
        target = cycle_array[(place + offset) % chips]
        return lax.dynamic_index_in_dim(summed, target, 1, keepdims=False)

    right = left = None
    for step in reversed(range(1, chips // 2 + 1)):
        term = for_place(step)
        right = term if right is None else right.astype(jnp.float32) + term
        right = around(right.astype(jnp.bfloat16), 1)
        if step < chips // 2:
            term = for_place(chips - step)
            left = term if left is None else left.astype(jnp.float32) + term
            left = around(left.astype(jnp.bfloat16), -1)
    return (for_place(0) + right.astype(jnp.float32) + left.astype(jnp.float32)).astype(jnp.bfloat16)


def solution(mesh):
    return jax.shard_map(
        functools.partial(body, size=mesh.shape["seq"]),
        mesh=mesh,
        in_specs=(
            P("group", "seq"),
            P("seq"),
            P("seq", None),
            P("seq", None),
            P("seq", None),
            P("seq", None),
            P(None, ("group", "seq"), None),
        ),
        out_specs=P("group", "seq"),
        check_vma=False,
    )
```

```python
import functools
import math

import jax
import jax.numpy as jnp
from jax import lax
from jax.experimental import pallas as pl
from jax.experimental.pallas import tpu as pltpu
from jax.sharding import PartitionSpec as P

H = 64
KV = 8
DH = 128
EPS = 1e-05
PAD = 16
EARLY = 5
RELEASE = 1
MIB = 1 << 20
TRANS_B = (((1,), (1,)), ((), ()))


def in_vmem(count):
    return [pl.BlockSpec(memory_space=pltpu.VMEM)] * count


def anywhere(count):
    return [pl.BlockSpec(memory_space=pl.ANY)] * count


def cost(flops, moved):
    return pl.CostEstimate(flops=flops, bytes_accessed=moved, transcendentals=0)


def params(mib):
    return pltpu.CompilerParams(vmem_limit_bytes=mib * MIB)


def chip_at(place, chips):
    return jnp.where(place < chips // 2, 2 * place, 2 * (chips - 1 - place) + 1)


def place_of(chip, chips):
    return jnp.where(lax.rem(chip, 2) == 0, lax.div(chip, 2), chips - 1 - lax.div(chip, 2))


def here():
    device = lax.axis_index("seq")
    return lax.div(device, 2), lax.rem(device, 2)


def neighbour_chip(offset, chips):
    chip, _ = here()
    return chip_at(lax.rem(place_of(chip, chips) + offset + chips, chips), chips)


def pack_kernel(tokens, gain, block, sem):
    rows, width = tokens.shape
    copy = pltpu.make_async_copy(tokens, block.at[pl.ds(0, rows), :], sem)
    copy.start()
    wide = gain[...].astype(jnp.float32).reshape(1, width)
    block[rows:, :] = jnp.broadcast_to(wide, (PAD, width)).astype(jnp.bfloat16)
    copy.wait()


def pack(tokens, gain):
    rows, width = tokens.shape
    return pl.pallas_call(
        pack_kernel,
        out_shape=jax.ShapeDtypeStruct((rows + PAD, width), jnp.bfloat16),
        in_specs=anywhere(1) + in_vmem(1),
        out_specs=in_vmem(1)[0],
        scratch_shapes=[pltpu.SemaphoreType.DMA],
        name="pack",
    )(tokens, gain)


def cut_kernel(chips, cache, *pieces):
    chip, _ = here()
    for step, piece in enumerate(pieces):
        head = lax.div(lax.bitwise_xor(chip, step) * KV, chips)
        piece[...] = cache[:, :, pl.ds(pl.multiple_of(head * DH, DH), DH)]


def cut(cache, chips):
    shape = (2, cache.shape[1], DH)
    return pl.pallas_call(
        functools.partial(cut_kernel, chips),
        out_shape=[jax.ShapeDtypeStruct(shape, jnp.bfloat16)] * chips,
        in_specs=in_vmem(1),
        out_specs=in_vmem(chips),
        compiler_params=params(8),
        name="cut",
    )(cache)


def halve_kernel(chips, width, w_out, mine, send, sems):
    _, core = here()
    copies = []
    for side, half in enumerate((send, mine)):
        for offset in range(chips):
            column = 2 * neighbour_chip(offset, chips) + (core if side else 1 - core)
            columns = pl.ds(pl.multiple_of(column * width, width), width)
            copy = pltpu.make_async_copy(w_out.at[:, columns], half.at[offset], sems.at[side, offset])
            copy.start()
            copies.append(copy)
    for copy in copies:
        copy.wait()


def halve(w_out, chips):
    rows, columns = w_out.shape
    width = columns // (2 * chips)
    return pl.pallas_call(
        functools.partial(halve_kernel, chips, width),
        out_shape=[jax.ShapeDtypeStruct((chips, rows, width), jnp.bfloat16)] * 2,
        in_specs=anywhere(1),
        out_specs=in_vmem(2),
        scratch_shapes=[pltpu.SemaphoreType.DMA((2, chips))],
        compiler_params=params(12),
        name="halve",
    )(w_out)


def project_kernel(offsets, chips, rows, *refs):
    count = len(offsets)
    blocks = refs[:count]
    w_query, w_key, w_value, query_ref, own_ref, held, held_own, sems, own_sems = refs[count:]
    width = blocks[0].shape[1]
    _, core = here()
    half = w_key.shape[0]
    own_copies = [
        pltpu.make_async_copy(w_key, held_own.at[pl.ds(0, half), :], own_sems.at[0]),
        pltpu.make_async_copy(w_value, held_own.at[pl.ds(half, half), :], own_sems.at[1]),
    ]
    for copy in own_copies:
        copy.start()
    columns, copies = [], []
    for number, (offset, other) in enumerate(offsets):
        side = 1 - core if other else core
        owner = 2 * neighbour_chip(offset, chips) + side
        columns.append(pl.ds(pl.multiple_of(owner * width, width), width))
        copy = pltpu.make_async_copy(w_query.at[:, columns[number]], held.at[number], sems.at[number])
        copy.start()
        copies.append(copy)
    total = jnp.zeros((rows, 128), jnp.float32)
    for block in blocks:
        wide = block[:rows, :].astype(jnp.float32)
        square = wide * wide
        for lane in range(0, width, 128):
            total += square[:, lane : lane + 128]
    inverse = lax.rsqrt(jnp.sum(total, axis=1, keepdims=True) / (width * count) + EPS)
    query = jnp.zeros(query_ref.shape, jnp.float32)
    own = jnp.zeros(own_ref.shape, jnp.float32)
    for copy in own_copies:
        copy.wait()
    for number, block in enumerate(blocks):
        gain = block[rows : rows + PAD, :].astype(jnp.float32)[0:1, :]
        wide = block[:rows, :].astype(jnp.float32)
        normed = (wide * inverse * gain).astype(jnp.bfloat16)
        own += lax.dot_general(normed, held_own[:, columns[number]], TRANS_B, preferred_element_type=jnp.float32)
        copies[number].wait()
        query += lax.dot_general(normed, held[number], TRANS_B, preferred_element_type=jnp.float32)
    query_ref[...] = query.astype(jnp.bfloat16)
    own_ref[...] = own.astype(jnp.bfloat16)


def project(offsets, chips, blocks, w_query, w_key, w_value, rows):
    count, width = len(blocks), blocks[0].shape[1]
    return pl.pallas_call(
        functools.partial(project_kernel, offsets, chips, rows),
        out_shape=(
            jax.ShapeDtypeStruct((rows, w_query.shape[0]), jnp.bfloat16),
            jax.ShapeDtypeStruct((rows, 2 * w_key.shape[0]), jnp.bfloat16),
        ),
        in_specs=in_vmem(count) + anywhere(3),
        out_specs=tuple(in_vmem(2)),
        scratch_shapes=[
            pltpu.VMEM((count, w_query.shape[0], width), jnp.bfloat16),
            pltpu.VMEM((2 * w_key.shape[0], w_key.shape[1]), jnp.bfloat16),
            pltpu.SemaphoreType.DMA((count,)),
            pltpu.SemaphoreType.DMA((2,)),
        ],
        compiler_params=params(24),
        cost_estimate=cost(8 * rows * w_query.size, 2 * w_query.size),
        name="project",
    )(*blocks, w_query, w_key, w_value)


def attend_kernel(count, parts, heads, *refs):
    caches, owns = refs[:count], refs[count : count + parts]
    query_ref, out_ref, query_all, scores = refs[count + parts :]
    rows = query_ref.shape[0]
    half = owns[0].shape[1] // 2
    scale = 1.0 / math.sqrt(DH)
    _, core = here()
    own_parts = [own[...].astype(jnp.float32) for own in owns]
    if parts == 2:
        own_parts = [jnp.where(core == 0, own_parts[i], own_parts[1 - i]) for i in range(2)]
    own_key = jnp.concatenate([part[:, :half] for part in own_parts], axis=1)
    own_value = jnp.concatenate([part[:, half:] for part in own_parts], axis=1)
    for head in range(heads):
        query_all[head * rows : (head + 1) * rows, :] = query_ref[:, head * DH : (head + 1) * DH]
    query = query_all[...]
    keys_own = jnp.concatenate([own_key] * heads, axis=0)
    values_own = jnp.concatenate([own_value] * heads, axis=0)
    own = jnp.sum(query.astype(jnp.float32) * keys_own, axis=1, keepdims=True) * scale
    step = caches[0].shape[1]
    best = None
    for number, cache in enumerate(caches):
        part = lax.dot_general(query, cache[0], TRANS_B, preferred_element_type=jnp.float32)
        scores[:, number * step : (number + 1) * step] = part
        for lane in range(0, step, 128):
            piece = part[:, lane : lane + 128]
            best = piece if best is None else jnp.maximum(best, piece)
    top = jnp.maximum(jnp.max(best, axis=1, keepdims=True) * scale, own)
    total = jnp.zeros((heads * rows, 128), jnp.float32)
    numerator = jnp.zeros((heads * rows, DH), jnp.float32)
    for number, cache in enumerate(caches):
        weights = jnp.exp(scores[:, number * step : (number + 1) * step] * scale - top)
        for lane in range(0, step, 128):
            total += weights[:, lane : lane + 128]
        numerator += jnp.dot(weights.astype(jnp.bfloat16), cache[1], preferred_element_type=jnp.float32)
    own_weight = jnp.exp(own - top)
    denominator = jnp.sum(total, axis=1, keepdims=True) + own_weight
    rounded = own_weight.astype(jnp.bfloat16).astype(jnp.float32)
    result = ((numerator + rounded * values_own) / denominator).astype(jnp.bfloat16)
    for head in range(heads):
        out_ref[:, head * DH : (head + 1) * DH] = result[head * rows : (head + 1) * rows, :]


def attend(caches, owns, query):
    count, rows = len(caches), query.shape[0]
    heads = query.shape[1] // DH
    positions = count * caches[0].shape[1]
    return pl.pallas_call(
        functools.partial(attend_kernel, count, len(owns), heads),
        out_shape=jax.ShapeDtypeStruct(query.shape, jnp.bfloat16),
        in_specs=in_vmem(count + len(owns) + 1),
        out_specs=in_vmem(1)[0],
        scratch_shapes=[
            pltpu.VMEM((heads * rows, DH), jnp.bfloat16),
            pltpu.VMEM((heads * rows, positions), jnp.float32),
        ],
        compiler_params=params(24),
        name="attend",
    )(*caches, *owns, query)


def near_kernel(attention, weights, out_ref):
    for offset in range(weights.shape[0]):
        out_ref[offset] = jnp.dot(attention[...], weights[offset], preferred_element_type=jnp.float32)


def near(attention, weights):
    chips, _, width = weights.shape
    return pl.pallas_call(
        near_kernel,
        out_shape=jax.ShapeDtypeStruct((chips, attention.shape[0], width), jnp.float32),
        in_specs=in_vmem(2),
        out_specs=in_vmem(1)[0],
        compiler_params=params(12),
        name="near",
    )(attention, weights)


def far_kernel(offsets, attention, weights, base, *outs):
    for out, offset in zip(outs, offsets):
        term = jnp.dot(attention[...], weights[offset], preferred_element_type=jnp.float32)
        out[...] = (base[offset] + term).astype(out.dtype)


def far(attention, weights, base, offsets, dtype):
    return pl.pallas_call(
        functools.partial(far_kernel, offsets),
        out_shape=[jax.ShapeDtypeStruct(base.shape[1:], dtype)] * len(offsets),
        in_specs=in_vmem(3),
        out_specs=in_vmem(len(offsets)),
        compiler_params=params(12),
        name="far",
    )(attention, weights, base)


def body(tokens, gain, w_query, w_key, w_value, w_out, prefix_cache, size):
    chips = size // 2
    outer = chips // 2
    cycle = [2 * a for a in range(outer)] + [2 * a + 1 for a in reversed(range(outer))]

    def around(value, step):
        pairs = [
            (2 * cycle[p] + k, 2 * cycle[(p + step) % chips] + k) for p in range(chips) for k in (0, 1)
        ]
        return lax.ppermute(value, "seq", pairs)

    def swap(value, bits):
        return lax.ppermute(value, "seq", [(i, i ^ bits) for i in range(size)])

    rows = tokens.shape[0]

    block = pack(tokens, gain)
    blocks, offsets = [], []

    def take(value, offset):
        blocks.extend([value, swap(value, 1)])
        offsets.extend([(offset, False), (offset, True)])

    take(block, 0)
    right = left = block
    reach = chips // 2
    for step in range(1, reach + 1):
        right = around(right, 1)
        if step == 1:
            w_out, right = lax.optimization_barrier((w_out, right))
        if step == min(2, reach):
            prefix_cache, right = lax.optimization_barrier((prefix_cache, right))
        if step == max(reach - RELEASE, 1):
            pieces = cut(prefix_cache, chips)
            *pieces, right = lax.optimization_barrier((*pieces, right))
        take(right, -step)
        if step < reach:
            left = around(left, -1)
            take(left, step)
    mine, send = halve(w_out, chips)
    w_other = swap(send, 1)
    query, own = project(tuple(offsets), chips, blocks, w_query, w_key, w_value, rows)

    order = list(range(chips // 2, chips)) + list(range(2, chips // 2)) + [1]
    order = [step for step in order if step < chips]
    parts = {}
    for number, step in enumerate(order):
        if number == EARLY:
            *pieces, query = lax.optimization_barrier((*pieces, query))
        parts[step] = swap(pieces[step], 2 * step)
    held = list(parts.values())
    *held, query = lax.optimization_barrier((*held, query))
    caches = [pieces[0], swap(pieces[0], 1)]
    for part in held:
        caches += [part, swap(part, 1)]

    sharers = size // KV
    if sharers == 1:
        owns = [own]
    elif sharers == 2:
        owns = [own, swap(own, 1)]
    else:
        groups = [list(range(g * sharers, (g + 1) * sharers)) for g in range(KV)]
        gathered = lax.all_gather(own, "seq", axis=0, axis_index_groups=groups)
        owns = [gathered[i] for i in range(sharers)]
    attention = attend(caches, owns, query)

    other = swap(attention, 1)
    base = near(attention, mine)
    first = [reach] + ([chips - reach + 1] if reach > 1 else [])
    rest = [offset for offset in range(chips) if offset not in first]
    terms = dict(zip(first, far(other, w_other, base, tuple(first), jnp.bfloat16)))
    terms.update(zip(rest, far(other, w_other, base, tuple(rest), jnp.float32)))
    right = left = None
    for step in reversed(range(1, reach + 1)):
        term = terms[step]
        right = term if right is None else (right.astype(jnp.float32) + term).astype(jnp.bfloat16)
        right = around(right, 1)
        if step < reach:
            term = terms[chips - step]
            left = term if left is None else (left.astype(jnp.float32) + term).astype(jnp.bfloat16)
            left = around(left, -1)
    total = terms[0] + right.astype(jnp.float32)
    if left is not None:
        total += left.astype(jnp.float32)
    return total.astype(jnp.bfloat16)


def solution(mesh):
    return jax.shard_map(
        functools.partial(body, size=mesh.shape["seq"]),
        mesh=mesh,
        in_specs=(
            P("group", "seq"),
            P("seq"),
            P("seq", None),
            P("seq", None),
            P("seq", None),
            P("seq", None),
            P(None, ("group", "seq"), None),
        ),
        out_specs=P("group", "seq"),
        check_vma=False,
    )
```

```python
import functools
import math

import jax
import jax.numpy as jnp
from jax import lax
from jax.experimental import pallas as pl
from jax.experimental.pallas import tpu as pltpu
from jax.sharding import PartitionSpec as P

H = 64
KV = 8
DH = 128
EPS = 1e-05
PAD = 16
MIB = 1 << 20
TRANS_B = (((1,), (1,)), ((), ()))


def in_vmem(count):
    return [pl.BlockSpec(memory_space=pltpu.VMEM)] * count


def anywhere(count):
    return [pl.BlockSpec(memory_space=pl.ANY)] * count


def cost(flops, moved):
    return pl.CostEstimate(flops=flops, bytes_accessed=moved, transcendentals=0)


def params(mib):
    return pltpu.CompilerParams(vmem_limit_bytes=mib * MIB)


def chip_at(place, chips):
    return jnp.where(place < chips // 2, 2 * place, 2 * (chips - 1 - place) + 1)


def place_of(chip, chips):
    return jnp.where(lax.rem(chip, 2) == 0, lax.div(chip, 2), chips - 1 - lax.div(chip, 2))


def here():
    device = lax.axis_index("seq")
    return lax.div(device, 2), lax.rem(device, 2)


def neighbour_chip(offset, chips):
    chip, _ = here()
    return chip_at(lax.rem(place_of(chip, chips) + offset + chips, chips), chips)


def pack_kernel(tokens, gain, block, sem):
    rows, width = tokens.shape
    copy = pltpu.make_async_copy(tokens, block.at[pl.ds(0, rows), :], sem)
    copy.start()
    wide = gain[...].astype(jnp.float32).reshape(1, width)
    block[rows:, :] = jnp.broadcast_to(wide, (PAD, width)).astype(jnp.bfloat16)
    copy.wait()


def pack(tokens, gain):
    rows, width = tokens.shape
    return pl.pallas_call(
        pack_kernel,
        out_shape=pltpu.VMEM((rows + PAD, width), jnp.bfloat16),
        in_specs=anywhere(1) + in_vmem(1),
        out_specs=in_vmem(1)[0],
        scratch_shapes=[pltpu.SemaphoreType.DMA],
        name="pack",
    )(tokens, gain)


def cut_kernel(chips, cache, *pieces):
    chip, _ = here()
    for step, piece in enumerate(pieces):
        head = lax.div(lax.bitwise_xor(chip, step) * KV, chips)
        piece[...] = cache[:, :, pl.ds(pl.multiple_of(head * DH, DH), DH)]


def cut(cache, chips):
    shape = (2, cache.shape[1], DH)
    return pl.pallas_call(
        functools.partial(cut_kernel, chips),
        out_shape=[jax.ShapeDtypeStruct(shape, jnp.bfloat16)] * chips,
        in_specs=in_vmem(1),
        out_specs=in_vmem(chips),
        compiler_params=params(8),
        name="cut",
    )(cache)


def half_kernel(groups, chips, width, w_out, *refs):
    outs, sems = refs[:-1], refs[-1]
    _, core = here()
    copies = []
    for out, (mine, offsets) in zip(outs, groups):
        for number, offset in enumerate(offsets):
            column = 2 * neighbour_chip(offset, chips) + (core if mine else 1 - core)
            columns = pl.ds(pl.multiple_of(column * width, width), width)
            copy = pltpu.make_async_copy(w_out.at[:, columns], out.at[number], sems.at[len(copies)])
            copy.start()
            copies.append(copy)
    for copy in copies:
        copy.wait()


def in_hbm(value):
    return pltpu.with_memory_space_constraint(value, pltpu.HBM)


def half(w_out, chips, *groups):
    rows, columns = w_out.shape
    width = columns // (2 * chips)
    return pl.pallas_call(
        functools.partial(half_kernel, groups, chips, width),
        out_shape=[jax.ShapeDtypeStruct((len(offsets), rows, width), jnp.bfloat16) for _, offsets in groups],
        in_specs=anywhere(1),
        out_specs=in_vmem(len(groups)),
        scratch_shapes=[pltpu.SemaphoreType.DMA((sum(len(offsets) for _, offsets in groups),))],
        compiler_params=params(12),
        name="half",
    )(in_hbm(w_out))


def project_kernel(offsets, chips, rows, *refs):
    count = len(offsets)
    blocks = refs[:count]
    w_query, w_key, w_value, query_ref, own_ref, held, held_own, sems, own_sems = refs[count:]
    width = blocks[0].shape[1]
    side = w_key.shape[0]
    _, core = here()
    own_copies = [
        pltpu.make_async_copy(w_key, held_own.at[pl.ds(0, side), :], own_sems.at[0]),
        pltpu.make_async_copy(w_value, held_own.at[pl.ds(side, side), :], own_sems.at[1]),
    ]
    for copy in own_copies:
        copy.start()
    columns, copies = [], []
    for number, (offset, other) in enumerate(offsets):
        owner = 2 * neighbour_chip(offset, chips) + (1 - core if other else core)
        columns.append(pl.ds(pl.multiple_of(owner * width, width), width))
        copy = pltpu.make_async_copy(w_query.at[:, columns[number]], held.at[number], sems.at[number])
        copy.start()
        copies.append(copy)
    total = jnp.zeros((rows, 128), jnp.float32)
    for block in blocks:
        wide = block[:rows, :].astype(jnp.float32)
        square = wide * wide
        for lane in range(0, width, 128):
            total += square[:, lane : lane + 128]
    inverse = lax.rsqrt(jnp.sum(total, axis=1, keepdims=True) / (width * count) + EPS)
    query = jnp.zeros(query_ref.shape, jnp.float32)
    own = jnp.zeros(own_ref.shape, jnp.float32)
    for copy in own_copies:
        copy.wait()
    for number, block in enumerate(blocks):
        gain = block[rows : rows + PAD, :].astype(jnp.float32)[0:1, :]
        wide = block[:rows, :].astype(jnp.float32)
        normed = (wide * inverse * gain).astype(jnp.bfloat16)
        own += lax.dot_general(normed, held_own[:, columns[number]], TRANS_B, preferred_element_type=jnp.float32)
        copies[number].wait()
        query += lax.dot_general(normed, held[number], TRANS_B, preferred_element_type=jnp.float32)
    query_ref[...] = query.astype(jnp.bfloat16)
    own_ref[...] = own.astype(jnp.bfloat16)


def project(offsets, chips, blocks, w_query, w_key, w_value, rows):
    count, width = len(blocks), blocks[0].shape[1]
    return pl.pallas_call(
        functools.partial(project_kernel, offsets, chips, rows),
        out_shape=(
            jax.ShapeDtypeStruct((rows, w_query.shape[0]), jnp.bfloat16),
            jax.ShapeDtypeStruct((rows, 2 * w_key.shape[0]), jnp.bfloat16),
        ),
        in_specs=in_vmem(count) + anywhere(3),
        out_specs=tuple(in_vmem(2)),
        scratch_shapes=[
            pltpu.VMEM((count, w_query.shape[0], width), jnp.bfloat16),
            pltpu.VMEM((2 * w_key.shape[0], w_key.shape[1]), jnp.bfloat16),
            pltpu.SemaphoreType.DMA((count,)),
            pltpu.SemaphoreType.DMA((2,)),
        ],
        compiler_params=params(24),
        name="project",
    )(*blocks, in_hbm(w_query), in_hbm(w_key), in_hbm(w_value))


def weigh(query, caches, scores, top, total, numerator):
    scale = 1.0 / math.sqrt(DH)
    step = caches[0].shape[1]
    best = None
    for number, cache in enumerate(caches):
        part = lax.dot_general(query, cache[0], TRANS_B, preferred_element_type=jnp.float32)
        scores[:, number * step : (number + 1) * step] = part
        for lane in range(0, step, 128):
            piece = part[:, lane : lane + 128]
            best = piece if best is None else jnp.maximum(best, piece)
    before = top
    top = jnp.maximum(jnp.max(best, axis=1, keepdims=True) * scale, top)
    shrink = jnp.exp(before - top)
    total, numerator = total * shrink, numerator * shrink
    for number, cache in enumerate(caches):
        weights = jnp.exp(scores[:, number * step : (number + 1) * step] * scale - top)
        for lane in range(0, step, 128):
            total += weights[:, lane : lane + 128]
        numerator += jnp.dot(weights.astype(jnp.bfloat16), cache[1], preferred_element_type=jnp.float32)
    return top, total, numerator


def begin_kernel(count, parts, heads, *refs):
    caches, owns = refs[:count], refs[count : count + parts]
    mine, other, query_all, top_ref, total_ref, numerator_ref, scores = refs[count + parts :]
    rows = mine.shape[0]
    lines = heads * rows
    side = owns[0].shape[1] // 2
    _, core = here()
    own_parts = [own[...].astype(jnp.float32) for own in owns]
    if parts == 2:
        own_parts = [jnp.where(core == 0, own_parts[i], own_parts[1 - i]) for i in range(2)]
    own_key = jnp.concatenate([part[:, :side] for part in own_parts], axis=1)
    own_value = jnp.concatenate([part[:, side:] for part in own_parts], axis=1)
    for number, query_ref in enumerate((mine, other)):
        for head in range(heads):
            start = number * lines + head * rows
            query_all[start : start + rows, :] = query_ref[:, head * DH : (head + 1) * DH]
    query = query_all[...]
    keys_own = jnp.concatenate([own_key] * (2 * heads), axis=0)
    own = jnp.sum(query.astype(jnp.float32) * keys_own, axis=1, keepdims=True) / math.sqrt(DH)
    lane = lax.broadcasted_iota(jnp.int32, (2 * lines, 128), 1)
    line = lax.broadcasted_iota(jnp.int32, (2 * lines, 128), 0)
    total = jnp.where((lane == 0) & (line < lines), 1.0, 0.0)
    numerator = jnp.concatenate([own_value] * heads + [jnp.zeros((lines, DH), jnp.float32)], axis=0)
    top, total, numerator = weigh(query, caches, scores, own, total, numerator)
    top_ref[...] = jnp.broadcast_to(top, top_ref.shape)
    total_ref[...] = total
    numerator_ref[...] = numerator


def begin(caches, owns, mine, other):
    count, rows = len(caches), mine.shape[0]
    heads = mine.shape[1] // DH
    lines = 2 * heads * rows
    positions = count * caches[0].shape[1]
    return pl.pallas_call(
        functools.partial(begin_kernel, count, len(owns), heads),
        out_shape=[jax.ShapeDtypeStruct((lines, DH), jnp.bfloat16)]
        + [jax.ShapeDtypeStruct((lines, 128), jnp.float32)] * 3,
        in_specs=in_vmem(count + len(owns) + 2),
        out_specs=in_vmem(4),
        scratch_shapes=[pltpu.VMEM((lines, positions), jnp.float32)],
        compiler_params=params(24),
        cost_estimate=cost(1, 1),
        name="begin",
    )(*caches, *owns, mine, other)


def finish_kernel(count, *refs):
    caches = refs[:count]
    query_all, top_ref, total_ref, numerator_ref, state_ref, sum_ref, scores = refs[count:]
    top, total, numerator = weigh(
        query_all[...], caches, scores, top_ref[:, 0:1], total_ref[...], numerator_ref[...]
    )
    lane = lax.broadcasted_iota(jnp.int32, total.shape, 1)
    state_ref[...] = jnp.where(lane < 64, top, jnp.sum(total, axis=1, keepdims=True))
    sum_ref[...] = numerator


def finish(caches, state):
    count = len(caches)
    lines = state[0].shape[0]
    positions = count * caches[0].shape[1]
    return pl.pallas_call(
        functools.partial(finish_kernel, count),
        out_shape=[jax.ShapeDtypeStruct((lines, 128), jnp.float32)] * 2,
        in_specs=in_vmem(count + 4),
        out_specs=in_vmem(2),
        scratch_shapes=[pltpu.VMEM((lines, positions), jnp.float32)],
        compiler_params=params(24),
        name="finish",
    )(*caches, *state)


def output_term(attention, weights):
    return sum(
        jnp.dot(part, weight, preferred_element_type=jnp.float32) for part, weight in zip(attention, weights)
    )


def merge_kernel(rows, *refs):
    state, sums, far_state, far_sums, mine, other = refs[:6]
    attention_ref, outs = refs[6], refs[7:]
    lines = state.shape[0] // 2
    heads = lines // rows
    parts = []
    for number in range(2):
        near_lines = slice(number * lines, (number + 1) * lines)
        far_lines = slice((1 - number) * lines, (2 - number) * lines)
        top, far_top = state[near_lines, 0:1], far_state[far_lines, 0:1]
        peak = jnp.maximum(top, far_top)
        scale, far_scale = jnp.exp(top - peak), jnp.exp(far_top - peak)
        denominator = state[near_lines, 64:65] * scale + far_state[far_lines, 64:65] * far_scale
        numerator = sums[near_lines, :] * scale + far_sums[far_lines, :] * far_scale
        result = (numerator / denominator).astype(jnp.bfloat16)
        for head in range(heads):
            attention_ref[number, :, head * DH : (head + 1) * DH] = result[head * rows : (head + 1) * rows, :]
        parts.append(attention_ref[number])
    for number, out in enumerate(outs):
        out[...] = output_term(parts, (mine[number], other[number])).astype(out.dtype)


def merge(state, sums, far_state, far_sums, mine, other, rows):
    count, depth, width = mine.shape
    return pl.pallas_call(
        functools.partial(merge_kernel, rows),
        out_shape=[jax.ShapeDtypeStruct((2, rows, depth), jnp.bfloat16)]
        + [jax.ShapeDtypeStruct((rows, width), jnp.bfloat16)] * count,
        in_specs=in_vmem(6),
        out_specs=in_vmem(1 + count),
        compiler_params=params(16),
        name="merge",
    )(state, sums, far_state, far_sums, mine, other)


def rest_kernel(attention, mine, other, *outs):
    for number, out in enumerate(outs):
        out[...] = output_term((attention[0], attention[1]), (mine[number], other[number]))


def rest(attention, mine, other):
    count, _, width = mine.shape
    return pl.pallas_call(
        rest_kernel,
        out_shape=[jax.ShapeDtypeStruct((attention.shape[1], width), jnp.float32)] * count,
        in_specs=in_vmem(3),
        out_specs=in_vmem(count),
        compiler_params=params(12),
        name="rest",
    )(attention, mine, other)


def body(tokens, gain, w_query, w_key, w_value, w_out, prefix_cache, size):
    chips = size // 2
    outer = chips // 2
    cycle = [2 * a for a in range(outer)] + [2 * a + 1 for a in reversed(range(outer))]

    def around(value, step):
        pairs = [
            (2 * cycle[p] + k, 2 * cycle[(p + step) % chips] + k) for p in range(chips) for k in (0, 1)
        ]
        return lax.ppermute(value, "seq", pairs)

    def swap(value, bits):
        return lax.ppermute(value, "seq", [(i, i ^ bits) for i in range(size)])

    rows = tokens.shape[0]

    block = pack(tokens, gain)
    blocks, offsets = [], []

    def take(value, offset):
        blocks.extend([value, swap(value, 1)])
        offsets.extend([(offset, False), (offset, True)])

    right = left = block
    reach = chips // 2
    take(block, 0)
    for step in range(1, reach + 1):
        right = around(right, 1)
        if step == min(2, reach):
            prefix_cache, right = lax.optimization_barrier((prefix_cache, right))
        if step == max(reach - 1, 1):
            pieces = cut(prefix_cache, chips)
            pieces, right = lax.optimization_barrier((pieces, right))
        take(right, -step)
        if step < reach:
            left = around(left, -1)
            take(left, step)

    parts = {step: swap(pieces[step], 2 * step) for step in [*range(reach, chips), *range(1, reach)]}
    query, own = project(tuple(offsets), chips, blocks, w_query, w_key, w_value, rows)

    sharers = size // KV
    other_query = swap(query, 1)
    if sharers == 2:
        owns = [own, swap(own, 1)]
    else:
        groups = [list(range(g * sharers, (g + 1) * sharers)) for g in range(KV)]
        gathered = lax.all_gather(own, "seq", axis=0, axis_index_groups=groups)
        owns = [gathered[i] for i in range(sharers)]

    first = tuple([reach] + ([chips - reach + 1] if reach > 1 else []))
    others = tuple(offset for offset in range(chips) if offset not in first)
    w_out, query = lax.optimization_barrier((w_out, query))
    send_first, send_others, mine_first, mine_others = half(
        w_out, chips, (False, first), (False, others), (True, first), (True, others)
    )
    other_first = swap(send_first, 1)
    far_parts = [parts[step] for step in range(reach, chips)]
    send_others, far_parts, owns, other_query = lax.optimization_barrier(
        (send_others, far_parts, owns, other_query)
    )
    other_others = swap(send_others, 1)

    query, mine_first = lax.optimization_barrier((query, mine_first))
    state = begin(far_parts, owns, query, other_query)
    state, sums = finish([pieces[0]] + [parts[step] for step in range(1, reach)], state)

    attention, *terms = merge(state, sums, swap(state, 1), swap(sums, 1), mine_first, other_first, rows)
    terms = dict(zip(first, terms))
    terms.update(zip(others, rest(attention, mine_others, other_others)))
    right = left = None
    for step in reversed(range(1, reach + 1)):
        term = terms[step]
        right = term if right is None else (right.astype(jnp.float32) + term).astype(jnp.bfloat16)
        right = around(right, 1)
        if step < reach:
            term = terms[chips - step]
            left = term if left is None else (left.astype(jnp.float32) + term).astype(jnp.bfloat16)
            left = around(left, -1)
    total = terms[0] + right.astype(jnp.float32)
    if left is not None:
        total += left.astype(jnp.float32)
    return total.astype(jnp.bfloat16)


def solution(mesh):
    return jax.shard_map(
        functools.partial(body, size=mesh.shape["seq"]),
        mesh=mesh,
        in_specs=(
            P("group", "seq"),
            P("seq"),
            P("seq", None),
            P("seq", None),
            P("seq", None),
            P("seq", None),
            P(None, ("group", "seq"), None),
        ),
        out_specs=P("group", "seq"),
        check_vma=False,
    )
```

```python
import functools
import math

import jax
import jax.numpy as jnp
from jax import lax
from jax.experimental import pallas as pl
from jax.experimental.pallas import tpu as pltpu
from jax.sharding import PartitionSpec as P

H = 64
KV = 8
DH = 128
EPS = 1e-05
PAD = 16
MIB = 1 << 20
TRANS_B = (((1,), (1,)), ((), ()))


def in_vmem(count):
    return [pl.BlockSpec(memory_space=pltpu.VMEM)] * count


def anywhere(count):
    return [pl.BlockSpec(memory_space=pl.ANY)] * count


def cost(flops, moved):
    return pl.CostEstimate(flops=flops, bytes_accessed=moved, transcendentals=0)


def params(mib):
    return pltpu.CompilerParams(vmem_limit_bytes=mib * MIB)


def chip_at(place, chips):
    return jnp.where(place < chips // 2, 2 * place, 2 * (chips - 1 - place) + 1)


def place_of(chip, chips):
    return jnp.where(lax.rem(chip, 2) == 0, lax.div(chip, 2), chips - 1 - lax.div(chip, 2))


def here():
    device = lax.axis_index("seq")
    return lax.div(device, 2), lax.rem(device, 2)


def neighbour_chip(offset, chips):
    chip, _ = here()
    return chip_at(lax.rem(place_of(chip, chips) + offset + chips, chips), chips)


def pack_kernel(tokens, gain, block, sem):
    rows, width = tokens.shape
    copy = pltpu.make_async_copy(tokens, block.at[pl.ds(0, rows), :], sem)
    copy.start()
    wide = gain[...].astype(jnp.float32).reshape(1, width)
    block[rows:, :] = jnp.broadcast_to(wide, (PAD, width)).astype(jnp.bfloat16)
    copy.wait()


def pack(tokens, gain):
    rows, width = tokens.shape
    return pl.pallas_call(
        pack_kernel,
        out_shape=pltpu.VMEM((rows + PAD, width), jnp.bfloat16),
        in_specs=anywhere(1) + in_vmem(1),
        out_specs=in_vmem(1)[0],
        scratch_shapes=[pltpu.SemaphoreType.DMA],
        name="pack",
    )(tokens, gain)


def cut_kernel(chips, cache, *pieces):
    chip, _ = here()
    for step, piece in enumerate(pieces):
        head = lax.div(lax.bitwise_xor(chip, step) * KV, chips)
        piece[...] = cache[:, :, pl.ds(pl.multiple_of(head * DH, DH), DH)]


def cut(cache, chips):
    shape = (2, cache.shape[1], DH)
    return pl.pallas_call(
        functools.partial(cut_kernel, chips),
        out_shape=[jax.ShapeDtypeStruct(shape, jnp.bfloat16)] * chips,
        in_specs=in_vmem(1),
        out_specs=in_vmem(chips),
        compiler_params=params(8),
        name="cut",
    )(cache)


def half_kernel(groups, chips, width, w_out, *refs):
    outs, sems = refs[:-1], refs[-1]
    _, core = here()
    copies = []
    for out, (mine, offsets) in zip(outs, groups):
        for number, offset in enumerate(offsets):
            column = 2 * neighbour_chip(offset, chips) + (core if mine else 1 - core)
            columns = pl.ds(pl.multiple_of(column * width, width), width)
            copy = pltpu.make_async_copy(w_out.at[:, columns], out.at[number], sems.at[len(copies)])
            copy.start()
            copies.append(copy)
    for copy in copies:
        copy.wait()


def in_hbm(value):
    return pltpu.with_memory_space_constraint(value, pltpu.HBM)


def half(w_out, chips, *groups):
    rows, columns = w_out.shape
    width = columns // (2 * chips)
    return pl.pallas_call(
        functools.partial(half_kernel, groups, chips, width),
        out_shape=[jax.ShapeDtypeStruct((len(offsets), rows, width), jnp.bfloat16) for _, offsets in groups],
        in_specs=anywhere(1),
        out_specs=in_vmem(len(groups)),
        scratch_shapes=[pltpu.SemaphoreType.DMA((sum(len(offsets) for _, offsets in groups),))],
        compiler_params=params(12),
        name="half",
    )(in_hbm(w_out))


def fetch_kernel(start, size, source, target, sem):
    copy = pltpu.make_async_copy(source.at[pl.ds(start, size), :], target, sem)
    copy.start()
    copy.wait()


def fetch(value, start, size):
    return pl.pallas_call(
        functools.partial(fetch_kernel, start, size),
        out_shape=pltpu.VMEM((size, value.shape[1]), jnp.bfloat16),
        in_specs=anywhere(1),
        out_specs=in_vmem(1)[0],
        scratch_shapes=[pltpu.SemaphoreType.DMA],
        compiler_params=params(8),
        cost_estimate=cost(0, 4 * size * value.shape[1]),
        name="fetch",
    )(in_hbm(value))


def project_kernel(offsets, chips, rows, *refs):
    count = len(offsets)
    blocks = refs[:count]
    w_first, w_second, w_key, w_value, query_ref, own_ref, held_own, own_sems = refs[count:]
    width = blocks[0].shape[1]
    side, middle = w_key.shape[0], w_first.shape[0]
    _, core = here()
    own_copies = [
        pltpu.make_async_copy(w_key, held_own.at[pl.ds(0, side), :], own_sems.at[0]),
        pltpu.make_async_copy(w_value, held_own.at[pl.ds(side, side), :], own_sems.at[1]),
    ]
    for copy in own_copies:
        copy.start()
    total = jnp.zeros((rows, 128), jnp.float32)
    for block in blocks:
        wide = block[:rows, :].astype(jnp.float32)
        square = wide * wide
        for lane in range(0, width, 128):
            total += square[:, lane : lane + 128]
    inverse = lax.rsqrt(jnp.sum(total, axis=1, keepdims=True) / (width * count) + EPS)
    first = jnp.zeros((rows, middle), jnp.float32)
    second = jnp.zeros((rows, middle), jnp.float32)
    own = jnp.zeros(own_ref.shape, jnp.float32)
    for copy in own_copies:
        copy.wait()
    for block, (offset, other) in zip(blocks, offsets):
        owner = 2 * neighbour_chip(offset, chips) + (1 - core if other else core)
        columns = pl.ds(pl.multiple_of(owner * width, width), width)
        gain = block[rows : rows + PAD, :].astype(jnp.float32)[0:1, :]
        wide = block[:rows, :].astype(jnp.float32)
        normed = (wide * inverse * gain).astype(jnp.bfloat16)
        own += lax.dot_general(normed, held_own[:, columns], TRANS_B, preferred_element_type=jnp.float32)
        first += lax.dot_general(normed, w_first[:, columns], TRANS_B, preferred_element_type=jnp.float32)
        second += lax.dot_general(normed, w_second[:, columns], TRANS_B, preferred_element_type=jnp.float32)
    query_ref[:, :middle] = first.astype(jnp.bfloat16)
    query_ref[:, middle:] = second.astype(jnp.bfloat16)
    own_ref[...] = own.astype(jnp.bfloat16)


def project(offsets, chips, blocks, w_first, w_second, w_key, w_value, rows):
    count = len(blocks)
    return pl.pallas_call(
        functools.partial(project_kernel, offsets, chips, rows),
        out_shape=(
            jax.ShapeDtypeStruct((rows, 2 * w_first.shape[0]), jnp.bfloat16),
            jax.ShapeDtypeStruct((rows, 2 * w_key.shape[0]), jnp.bfloat16),
        ),
        in_specs=in_vmem(count + 2) + anywhere(2),
        out_specs=tuple(in_vmem(2)),
        scratch_shapes=[
            pltpu.VMEM((2 * w_key.shape[0], w_key.shape[1]), jnp.bfloat16),
            pltpu.SemaphoreType.DMA((2,)),
        ],
        compiler_params=params(12),
        name="project",
    )(*blocks, w_first, w_second, in_hbm(w_key), in_hbm(w_value))


def weigh(query, caches, scores, top, total, numerator):
    scale = 1.0 / math.sqrt(DH)
    step = caches[0].shape[1]
    best = None
    for number, cache in enumerate(caches):
        part = lax.dot_general(query, cache[0], TRANS_B, preferred_element_type=jnp.float32)
        scores[:, number * step : (number + 1) * step] = part
        for lane in range(0, step, 128):
            piece = part[:, lane : lane + 128]
            best = piece if best is None else jnp.maximum(best, piece)
    before = top
    top = jnp.maximum(jnp.max(best, axis=1, keepdims=True) * scale, top)
    shrink = jnp.exp(before - top)
    total, numerator = total * shrink, numerator * shrink
    for number, cache in enumerate(caches):
        weights = jnp.exp(scores[:, number * step : (number + 1) * step] * scale - top)
        for lane in range(0, step, 128):
            total += weights[:, lane : lane + 128]
        numerator += jnp.dot(weights.astype(jnp.bfloat16), cache[1], preferred_element_type=jnp.float32)
    return top, total, numerator


def begin_kernel(count, parts, heads, *refs):
    caches, owns = refs[:count], refs[count : count + parts]
    mine, other, query_all, top_ref, total_ref, numerator_ref, scores = refs[count + parts :]
    rows = mine.shape[0]
    lines = heads * rows
    side = owns[0].shape[1] // 2
    _, core = here()
    own_parts = [own[...].astype(jnp.float32) for own in owns]
    if parts == 2:
        own_parts = [jnp.where(core == 0, own_parts[i], own_parts[1 - i]) for i in range(2)]
    own_key = jnp.concatenate([part[:, :side] for part in own_parts], axis=1)
    own_value = jnp.concatenate([part[:, side:] for part in own_parts], axis=1)
    for number, query_ref in enumerate((mine, other)):
        for head in range(heads):
            start = number * lines + head * rows
            query_all[start : start + rows, :] = query_ref[:, head * DH : (head + 1) * DH]
    query = query_all[...]
    keys_own = jnp.concatenate([own_key] * (2 * heads), axis=0)
    own = jnp.sum(query.astype(jnp.float32) * keys_own, axis=1, keepdims=True) / math.sqrt(DH)
    lane = lax.broadcasted_iota(jnp.int32, (2 * lines, 128), 1)
    line = lax.broadcasted_iota(jnp.int32, (2 * lines, 128), 0)
    total = jnp.where((lane == 0) & (line < lines), 1.0, 0.0)
    numerator = jnp.concatenate([own_value] * heads + [jnp.zeros((lines, DH), jnp.float32)], axis=0)
    top, total, numerator = weigh(query, caches, scores, own, total, numerator)
    top_ref[...] = jnp.broadcast_to(top, top_ref.shape)
    total_ref[...] = total
    numerator_ref[...] = numerator


def begin(caches, owns, mine, other):
    count, rows = len(caches), mine.shape[0]
    heads = mine.shape[1] // DH
    lines = 2 * heads * rows
    positions = count * caches[0].shape[1]
    return pl.pallas_call(
        functools.partial(begin_kernel, count, len(owns), heads),
        out_shape=[jax.ShapeDtypeStruct((lines, DH), jnp.bfloat16)]
        + [jax.ShapeDtypeStruct((lines, 128), jnp.float32)] * 3,
        in_specs=in_vmem(count + len(owns) + 2),
        out_specs=in_vmem(4),
        scratch_shapes=[pltpu.VMEM((lines, positions), jnp.float32)],
        compiler_params=params(24),
        cost_estimate=cost(1, 1),
        name="begin",
    )(*caches, *owns, mine, other)


def finish_kernel(count, *refs):
    caches = refs[:count]
    query_all, top_ref, total_ref, numerator_ref, state_ref, sum_ref, scores = refs[count:]
    top, total, numerator = weigh(
        query_all[...], caches, scores, top_ref[:, 0:1], total_ref[...], numerator_ref[...]
    )
    lane = lax.broadcasted_iota(jnp.int32, total.shape, 1)
    state_ref[...] = jnp.where(lane < 64, top, jnp.sum(total, axis=1, keepdims=True))
    sum_ref[...] = numerator


def finish(caches, state):
    count = len(caches)
    lines = state[0].shape[0]
    positions = count * caches[0].shape[1]
    return pl.pallas_call(
        functools.partial(finish_kernel, count),
        out_shape=[jax.ShapeDtypeStruct((lines, 128), jnp.float32)] * 2,
        in_specs=in_vmem(count + 4),
        out_specs=in_vmem(2),
        scratch_shapes=[pltpu.VMEM((lines, positions), jnp.float32)],
        compiler_params=params(24),
        name="finish",
    )(*caches, *state)


def output_term(attention, weights):
    return sum(
        jnp.dot(part, weight, preferred_element_type=jnp.float32) for part, weight in zip(attention, weights)
    )


def merge_kernel(rows, *refs):
    state, sums, far_state, far_sums, mine, other = refs[:6]
    attention_ref, outs = refs[6], refs[7:]
    lines = state.shape[0] // 2
    heads = lines // rows
    parts = []
    for number in range(2):
        near_lines = slice(number * lines, (number + 1) * lines)
        far_lines = slice((1 - number) * lines, (2 - number) * lines)
        top, far_top = state[near_lines, 0:1], far_state[far_lines, 0:1]
        peak = jnp.maximum(top, far_top)
        scale, far_scale = jnp.exp(top - peak), jnp.exp(far_top - peak)
        denominator = state[near_lines, 64:65] * scale + far_state[far_lines, 64:65] * far_scale
        numerator = sums[near_lines, :] * scale + far_sums[far_lines, :] * far_scale
        result = (numerator / denominator).astype(jnp.bfloat16)
        for head in range(heads):
            attention_ref[number, :, head * DH : (head + 1) * DH] = result[head * rows : (head + 1) * rows, :]
        parts.append(attention_ref[number])
    for number, out in enumerate(outs):
        out[...] = output_term(parts, (mine[number], other[number])).astype(out.dtype)


def merge(state, sums, far_state, far_sums, mine, other, rows):
    count, depth, width = mine.shape
    return pl.pallas_call(
        functools.partial(merge_kernel, rows),
        out_shape=[jax.ShapeDtypeStruct((2, rows, depth), jnp.bfloat16)]
        + [jax.ShapeDtypeStruct((rows, width), jnp.bfloat16)] * count,
        in_specs=in_vmem(6),
        out_specs=in_vmem(1 + count),
        compiler_params=params(16),
        name="merge",
    )(state, sums, far_state, far_sums, mine, other)


def rest_kernel(attention, mine, other, *outs):
    for number, out in enumerate(outs):
        out[...] = output_term((attention[0], attention[1]), (mine[number], other[number]))


def rest(attention, mine, other):
    count, _, width = mine.shape
    return pl.pallas_call(
        rest_kernel,
        out_shape=[jax.ShapeDtypeStruct((attention.shape[1], width), jnp.float32)] * count,
        in_specs=in_vmem(3),
        out_specs=in_vmem(count),
        compiler_params=params(12),
        name="rest",
    )(attention, mine, other)


def body(tokens, gain, w_query, w_key, w_value, w_out, prefix_cache, size):
    chips = size // 2
    outer = chips // 2
    cycle = [2 * a for a in range(outer)] + [2 * a + 1 for a in reversed(range(outer))]

    def around(value, step):
        pairs = [
            (2 * cycle[p] + k, 2 * cycle[(p + step) % chips] + k) for p in range(chips) for k in (0, 1)
        ]
        return lax.ppermute(value, "seq", pairs)

    def swap(value, bits):
        return lax.ppermute(value, "seq", [(i, i ^ bits) for i in range(size)])

    rows = tokens.shape[0]

    block = pack(tokens, gain)
    blocks, offsets = [], []

    def take(value, offset):
        blocks.extend([value, swap(value, 1)])
        offsets.extend([(offset, False), (offset, True)])

    right = left = block
    reach = chips // 2
    take(block, 0)
    middle = w_query.shape[0] // 2
    weights = []
    first = tuple([reach] + ([chips - reach + 1] if reach > 1 else []))
    others = tuple(offset for offset in range(chips) if offset not in first)
    for step in range(1, reach + 1):
        if step > 1:
            right, weights = lax.optimization_barrier((right, weights))
        if step <= 2:
            w_query, right = lax.optimization_barrier((w_query, right))
            weights = [*weights, fetch(w_query, (step - 1) * middle, middle)]
        if step == min(3, reach):
            w_out, right = lax.optimization_barrier((w_out, right))
            sends = half(w_out, chips, (False, first), (False, others))
        if step == reach and reach > 3:
            sends, right = lax.optimization_barrier((sends, right))
        right = around(right, 1)
        if step == 1:
            prefix_cache, right = lax.optimization_barrier((prefix_cache, right))
            pieces = cut(prefix_cache, chips)
        if step == min(2, reach):
            pieces, right = lax.optimization_barrier((pieces, right))
        if step == max(reach - 1, 1):
            pieces, right = lax.optimization_barrier((pieces, right))
        take(right, -step)
        if step < reach:
            left = around(left, -1)
            take(left, step)

    close = [swap(pieces[step], 2 * step) for step in range(1, reach)]
    soon = (chips - reach) // 2
    far_parts = [swap(pieces[step], 2 * step) for step in range(reach, reach + soon)]
    pieces, close, far_parts = lax.optimization_barrier((pieces, close, far_parts))
    far_parts += [swap(pieces[step], 2 * step) for step in range(reach + soon, chips)]
    query, own = project(tuple(offsets), chips, blocks, *weights, w_key, w_value, rows)

    sharers = size // KV
    other_query = swap(query, 1)
    if sharers == 2:
        owns = [own, swap(own, 1)]
    else:
        groups = [list(range(g * sharers, (g + 1) * sharers)) for g in range(KV)]
        gathered = lax.all_gather(own, "seq", axis=0, axis_index_groups=groups)
        owns = [gathered[i] for i in range(sharers)]

    send_first, send_others = sends
    other_first = swap(send_first, 1)
    send_others, owns, other_query, far_parts[:soon] = lax.optimization_barrier(
        (send_others, owns, other_query, far_parts[:soon])
    )
    other_others = swap(send_others, 1)
    state = begin([pieces[0], *close, *far_parts[:soon]], owns, query, other_query)
    w_out, state = lax.optimization_barrier((w_out, state))
    mine_first, mine_others = half(w_out, chips, (True, first), (True, others))
    state, mine_first, mine_others = lax.optimization_barrier((state, mine_first, mine_others))
    state, sums = finish(far_parts[soon:], state)

    attention, *terms = merge(state, sums, swap(state, 1), swap(sums, 1), mine_first, other_first, rows)
    terms = dict(zip(first, terms))
    terms.update(zip(others, rest(attention, mine_others, other_others)))
    right = left = None
    for step in reversed(range(1, reach + 1)):
        term = terms[step]
        right = term if right is None else (right.astype(jnp.float32) + term).astype(jnp.bfloat16)
        right = around(right, 1)
        if step < reach:
            term = terms[chips - step]
            left = term if left is None else (left.astype(jnp.float32) + term).astype(jnp.bfloat16)
            left = around(left, -1)
    total = terms[0] + right.astype(jnp.float32)
    if left is not None:
        total += left.astype(jnp.float32)
    return total.astype(jnp.bfloat16)


def solution(mesh):
    return jax.shard_map(
        functools.partial(body, size=mesh.shape["seq"]),
        mesh=mesh,
        in_specs=(
            P("group", "seq"),
            P("seq"),
            P("seq", None),
            P("seq", None),
            P("seq", None),
            P("seq", None),
            P(None, ("group", "seq"), None),
        ),
        out_specs=P("group", "seq"),
        check_vma=False,
    )
```

```python
import functools
import math

import jax
import jax.numpy as jnp
from jax import lax
from jax.experimental import pallas as pl
from jax.experimental.pallas import tpu as pltpu
from jax.sharding import PartitionSpec as P

H = 64
KV = 8
DH = 128
EPS = 1e-05
PAD = 16
MIB = 1 << 20
TRANS_B = (((1,), (1,)), ((), ()))


def in_vmem(count):
    return [pl.BlockSpec(memory_space=pltpu.VMEM)] * count


def anywhere(count):
    return [pl.BlockSpec(memory_space=pl.ANY)] * count


def cost(flops, moved):
    return pl.CostEstimate(flops=flops, bytes_accessed=moved, transcendentals=0)


def params(mib):
    return pltpu.CompilerParams(vmem_limit_bytes=mib * MIB)


def chip_at(place, chips):
    return jnp.where(place < chips // 2, 2 * place, 2 * (chips - 1 - place) + 1)


def place_of(chip, chips):
    return jnp.where(lax.rem(chip, 2) == 0, lax.div(chip, 2), chips - 1 - lax.div(chip, 2))


def here():
    device = lax.axis_index("seq")
    return lax.div(device, 2), lax.rem(device, 2)


def neighbour_chip(offset, chips):
    chip, _ = here()
    return chip_at(lax.rem(place_of(chip, chips) + offset + chips, chips), chips)


def pack_kernel(tokens, gain, block, sem):
    rows, width = tokens.shape
    copy = pltpu.make_async_copy(tokens, block.at[pl.ds(0, rows), :], sem)
    copy.start()
    wide = gain[...].astype(jnp.float32).reshape(1, width)
    block[rows:, :] = jnp.broadcast_to(wide, (PAD, width)).astype(jnp.bfloat16)
    copy.wait()


def pack(tokens, gain):
    rows, width = tokens.shape
    return pl.pallas_call(
        pack_kernel,
        out_shape=pltpu.VMEM((rows + PAD, width), jnp.bfloat16),
        in_specs=anywhere(1) + in_vmem(1),
        out_specs=in_vmem(1)[0],
        scratch_shapes=[pltpu.SemaphoreType.DMA],
        name="pack",
    )(tokens, gain)


def cut_kernel(chips, cache, *pieces):
    chip, _ = here()
    for step, piece in enumerate(pieces):
        head = lax.div(lax.bitwise_xor(chip, step) * KV, chips)
        piece[...] = cache[:, :, pl.ds(pl.multiple_of(head * DH, DH), DH)]


def cut(cache, chips):
    shape = (2, cache.shape[1], DH)
    return pl.pallas_call(
        functools.partial(cut_kernel, chips),
        out_shape=[jax.ShapeDtypeStruct(shape, jnp.bfloat16)] * chips,
        in_specs=in_vmem(1),
        out_specs=in_vmem(chips),
        compiler_params=params(8),
        name="cut",
    )(cache)


def half_kernel(groups, chips, width, w_out, *refs):
    outs, sems = refs[:-1], refs[-1]
    _, core = here()
    copies = []
    for out, (mine, offsets) in zip(outs, groups):
        for number, offset in enumerate(offsets):
            column = 2 * neighbour_chip(offset, chips) + (core if mine else 1 - core)
            columns = pl.ds(pl.multiple_of(column * width, width), width)
            copy = pltpu.make_async_copy(w_out.at[:, columns], out.at[number], sems.at[len(copies)])
            copy.start()
            copies.append(copy)
    for copy in copies:
        copy.wait()


def in_hbm(value):
    return pltpu.with_memory_space_constraint(value, pltpu.HBM)


def half(w_out, chips, *groups):
    rows, columns = w_out.shape
    width = columns // (2 * chips)
    return pl.pallas_call(
        functools.partial(half_kernel, groups, chips, width),
        out_shape=[jax.ShapeDtypeStruct((len(offsets), rows, width), jnp.bfloat16) for _, offsets in groups],
        in_specs=anywhere(1),
        out_specs=in_vmem(len(groups)),
        scratch_shapes=[pltpu.SemaphoreType.DMA((sum(len(offsets) for _, offsets in groups),))],
        compiler_params=params(12),
        name="half",
    )(in_hbm(w_out))


def fetch_kernel(start, size, source, target, sem):
    copy = pltpu.make_async_copy(source.at[pl.ds(start, size), :], target, sem)
    copy.start()
    copy.wait()


def fetch(value, start, size):
    return pl.pallas_call(
        functools.partial(fetch_kernel, start, size),
        out_shape=pltpu.VMEM((size, value.shape[1]), jnp.bfloat16),
        in_specs=anywhere(1),
        out_specs=in_vmem(1)[0],
        scratch_shapes=[pltpu.SemaphoreType.DMA],
        compiler_params=params(8),
        cost_estimate=cost(0, 4 * size * value.shape[1]),
        name="fetch",
    )(in_hbm(value))


def project_kernel(offsets, chips, rows, *refs):
    count = len(offsets)
    blocks = refs[:count]
    w_first, w_second, w_key, w_value, query_ref, own_ref, held_own, own_sems = refs[count:]
    width = blocks[0].shape[1]
    side, middle = w_key.shape[0], w_first.shape[0]
    _, core = here()
    own_copies = [
        pltpu.make_async_copy(w_key, held_own.at[pl.ds(0, side), :], own_sems.at[0]),
        pltpu.make_async_copy(w_value, held_own.at[pl.ds(side, side), :], own_sems.at[1]),
    ]
    for copy in own_copies:
        copy.start()
    total = jnp.zeros((rows, 128), jnp.float32)
    for block in blocks:
        wide = block[:rows, :].astype(jnp.float32)
        square = wide * wide
        for lane in range(0, width, 128):
            total += square[:, lane : lane + 128]
    inverse = lax.rsqrt(jnp.sum(total, axis=1, keepdims=True) / (width * count) + EPS)
    first = jnp.zeros((rows, middle), jnp.float32)
    second = jnp.zeros((rows, middle), jnp.float32)
    own = jnp.zeros(own_ref.shape, jnp.float32)
    for copy in own_copies:
        copy.wait()
    for block, (offset, other) in zip(blocks, offsets):
        owner = 2 * neighbour_chip(offset, chips) + (1 - core if other else core)
        columns = pl.ds(pl.multiple_of(owner * width, width), width)
        gain = block[rows : rows + PAD, :].astype(jnp.float32)[0:1, :]
        wide = block[:rows, :].astype(jnp.float32)
        normed = (wide * inverse * gain).astype(jnp.bfloat16)
        own += lax.dot_general(normed, held_own[:, columns], TRANS_B, preferred_element_type=jnp.float32)
        first += lax.dot_general(normed, w_first[:, columns], TRANS_B, preferred_element_type=jnp.float32)
        second += lax.dot_general(normed, w_second[:, columns], TRANS_B, preferred_element_type=jnp.float32)
    query_ref[:, :middle] = first.astype(jnp.bfloat16)
    query_ref[:, middle:] = second.astype(jnp.bfloat16)
    own_ref[...] = own.astype(jnp.bfloat16)


def project(offsets, chips, blocks, w_first, w_second, w_key, w_value, rows):
    count = len(blocks)
    return pl.pallas_call(
        functools.partial(project_kernel, offsets, chips, rows),
        out_shape=(
            jax.ShapeDtypeStruct((rows, 2 * w_first.shape[0]), jnp.bfloat16),
            jax.ShapeDtypeStruct((rows, 2 * w_key.shape[0]), jnp.bfloat16),
        ),
        in_specs=in_vmem(count + 2) + anywhere(2),
        out_specs=tuple(in_vmem(2)),
        scratch_shapes=[
            pltpu.VMEM((2 * w_key.shape[0], w_key.shape[1]), jnp.bfloat16),
            pltpu.SemaphoreType.DMA((2,)),
        ],
        compiler_params=params(12),
        name="project",
    )(*blocks, w_first, w_second, in_hbm(w_key), in_hbm(w_value))


def weigh(query, caches, scores, top, total, numerator):
    scale = 1.0 / math.sqrt(DH)
    step = caches[0].shape[1]
    best = None
    for number, cache in enumerate(caches):
        part = lax.dot_general(query, cache[0], TRANS_B, preferred_element_type=jnp.float32)
        scores[:, number * step : (number + 1) * step] = part
        for lane in range(0, step, 128):
            piece = part[:, lane : lane + 128]
            best = piece if best is None else jnp.maximum(best, piece)
    before = top
    top = jnp.maximum(jnp.max(best, axis=1, keepdims=True) * scale, top)
    shrink = jnp.exp(before - top)
    total, numerator = total * shrink, numerator * shrink
    for number, cache in enumerate(caches):
        weights = jnp.exp(scores[:, number * step : (number + 1) * step] * scale - top)
        for lane in range(0, step, 128):
            total += weights[:, lane : lane + 128]
        numerator += jnp.dot(weights.astype(jnp.bfloat16), cache[1], preferred_element_type=jnp.float32)
    return top, total, numerator


def begin_kernel(count, parts, heads, *refs):
    caches, owns = refs[:count], refs[count : count + parts]
    mine, other, query_all, top_ref, total_ref, numerator_ref, scores = refs[count + parts :]
    rows = mine.shape[0]
    lines = heads * rows
    side = owns[0].shape[1] // 2
    _, core = here()
    own_parts = [own[...].astype(jnp.float32) for own in owns]
    if parts == 2:
        own_parts = [jnp.where(core == 0, own_parts[i], own_parts[1 - i]) for i in range(2)]
    own_key = jnp.concatenate([part[:, :side] for part in own_parts], axis=1)
    own_value = jnp.concatenate([part[:, side:] for part in own_parts], axis=1)
    for number, query_ref in enumerate((mine, other)):
        for head in range(heads):
            start = number * lines + head * rows
            query_all[start : start + rows, :] = query_ref[:, head * DH : (head + 1) * DH]
    query = query_all[...]
    keys_own = jnp.concatenate([own_key] * (2 * heads), axis=0)
    own = jnp.sum(query.astype(jnp.float32) * keys_own, axis=1, keepdims=True) / math.sqrt(DH)
    lane = lax.broadcasted_iota(jnp.int32, (2 * lines, 128), 1)
    line = lax.broadcasted_iota(jnp.int32, (2 * lines, 128), 0)
    total = jnp.where((lane == 0) & (line < lines), 1.0, 0.0)
    numerator = jnp.concatenate([own_value] * heads + [jnp.zeros((lines, DH), jnp.float32)], axis=0)
    top, total, numerator = weigh(query, caches, scores, own, total, numerator)
    top_ref[...] = jnp.broadcast_to(top, top_ref.shape)
    total_ref[...] = total
    numerator_ref[...] = numerator


def begin(caches, owns, mine, other):
    count, rows = len(caches), mine.shape[0]
    heads = mine.shape[1] // DH
    lines = 2 * heads * rows
    positions = count * caches[0].shape[1]
    return pl.pallas_call(
        functools.partial(begin_kernel, count, len(owns), heads),
        out_shape=[jax.ShapeDtypeStruct((lines, DH), jnp.bfloat16)]
        + [jax.ShapeDtypeStruct((lines, 128), jnp.float32)] * 3,
        in_specs=in_vmem(count + len(owns) + 2),
        out_specs=in_vmem(4),
        scratch_shapes=[pltpu.VMEM((lines, positions), jnp.float32)],
        compiler_params=params(24),
        cost_estimate=cost(1, 1),
        name="begin",
    )(*caches, *owns, mine, other)


def finish_kernel(count, *refs):
    caches = refs[:count]
    query_all, top_ref, total_ref, numerator_ref, state_ref, sum_ref, scores = refs[count:]
    top, total, numerator = weigh(
        query_all[...], caches, scores, top_ref[:, 0:1], total_ref[...], numerator_ref[...]
    )
    lane = lax.broadcasted_iota(jnp.int32, total.shape, 1)
    state_ref[...] = jnp.where(lane < 64, top, jnp.sum(total, axis=1, keepdims=True))
    sum_ref[...] = numerator


def finish(caches, state):
    count = len(caches)
    lines = state[0].shape[0]
    positions = count * caches[0].shape[1]
    return pl.pallas_call(
        functools.partial(finish_kernel, count),
        out_shape=[jax.ShapeDtypeStruct((lines, 128), jnp.float32)] * 2,
        in_specs=in_vmem(count + 4),
        out_specs=in_vmem(2),
        scratch_shapes=[pltpu.VMEM((lines, positions), jnp.float32)],
        compiler_params=params(24),
        name="finish",
    )(*caches, *state)


def output_term(attention, weights):
    return sum(
        jnp.dot(part, weight, preferred_element_type=jnp.float32) for part, weight in zip(attention, weights)
    )


def merge_kernel(rows, *refs):
    state, sums, far_state, far_sums, mine, other = refs[:6]
    attention_ref, outs = refs[6], refs[7:]
    lines = state.shape[0] // 2
    heads = lines // rows
    parts = []
    for number in range(2):
        near_lines = slice(number * lines, (number + 1) * lines)
        far_lines = slice((1 - number) * lines, (2 - number) * lines)
        top, far_top = state[near_lines, 0:1], far_state[far_lines, 0:1]
        peak = jnp.maximum(top, far_top)
        scale, far_scale = jnp.exp(top - peak), jnp.exp(far_top - peak)
        denominator = state[near_lines, 64:65] * scale + far_state[far_lines, 64:65] * far_scale
        numerator = sums[near_lines, :] * scale + far_sums[far_lines, :] * far_scale
        result = (numerator / denominator).astype(jnp.bfloat16)
        for head in range(heads):
            attention_ref[number, :, head * DH : (head + 1) * DH] = result[head * rows : (head + 1) * rows, :]
        parts.append(attention_ref[number])
    for number, out in enumerate(outs):
        out[...] = output_term(parts, (mine[number], other[number])).astype(out.dtype)


def merge(state, sums, far_state, far_sums, mine, other, rows):
    count, depth, width = mine.shape
    return pl.pallas_call(
        functools.partial(merge_kernel, rows),
        out_shape=[jax.ShapeDtypeStruct((2, rows, depth), jnp.bfloat16)]
        + [jax.ShapeDtypeStruct((rows, width), jnp.bfloat16)] * count,
        in_specs=in_vmem(6),
        out_specs=in_vmem(1 + count),
        compiler_params=params(16),
        name="merge",
    )(state, sums, far_state, far_sums, mine, other)


def rest_kernel(attention, mine, other, *outs):
    for number, out in enumerate(outs):
        out[...] = output_term((attention[0], attention[1]), (mine[number], other[number]))


def rest(attention, mine, other):
    count, _, width = mine.shape
    return pl.pallas_call(
        rest_kernel,
        out_shape=[jax.ShapeDtypeStruct((attention.shape[1], width), jnp.float32)] * count,
        in_specs=in_vmem(3),
        out_specs=in_vmem(count),
        compiler_params=params(12),
        name="rest",
    )(attention, mine, other)


def body(tokens, gain, w_query, w_key, w_value, w_out, prefix_cache, size):
    chips = size // 2
    outer = chips // 2
    cycle = [2 * a for a in range(outer)] + [2 * a + 1 for a in reversed(range(outer))]

    def around(value, step):
        pairs = [
            (2 * cycle[p] + k, 2 * cycle[(p + step) % chips] + k) for p in range(chips) for k in (0, 1)
        ]
        return lax.ppermute(value, "seq", pairs)

    def swap(value, bits):
        return lax.ppermute(value, "seq", [(i, i ^ bits) for i in range(size)])

    rows = tokens.shape[0]

    block = pack(tokens, gain)
    blocks, offsets = [], []

    def take(value, offset):
        blocks.extend([value, swap(value, 1)])
        offsets.extend([(offset, False), (offset, True)])

    right = left = block
    reach = chips // 2
    take(block, 0)
    middle = w_query.shape[0] // 2
    weights = []
    first = tuple([reach] + ([chips - reach + 1] if reach > 1 else []))
    others = tuple(offset for offset in range(chips) if offset not in first)
    for step in range(1, reach + 1):
        if step > 1:
            right, weights = lax.optimization_barrier((right, weights))
        if step <= 2:
            w_query, right = lax.optimization_barrier((w_query, right))
            weights = [*weights, fetch(w_query, (step - 1) * middle, middle)]
        right = around(right, 1)
        if step == 1:
            prefix_cache, right = lax.optimization_barrier((prefix_cache, right))
            pieces = cut(prefix_cache, chips)
        if step == min(2, reach):
            pieces, right = lax.optimization_barrier((pieces, right))
        if step == max(reach - 1, 1):
            pieces, right = lax.optimization_barrier((pieces, right))
        take(right, -step)
        if step < reach:
            left = around(left, -1)
            take(left, step)

    soon = (chips - reach) // 2
    sooner = [*range(reach, reach + soon), *range(1, reach)]
    later = [step for step in range(1, chips) if step not in sooner]
    close = [swap(pieces[step], 2 * step) for step in sooner]
    pieces, close = lax.optimization_barrier((pieces, close))
    far_parts = [swap(pieces[step], 2 * step) for step in later]
    query, own = project(tuple(offsets), chips, blocks, *weights, w_key, w_value, rows)

    w_out, query = lax.optimization_barrier((w_out, query))
    sends = half(w_out, chips, (False, first), (False, others))
    query, own, sends = lax.optimization_barrier((query, own, sends))

    sharers = size // KV
    other_query = swap(query, 1)
    if sharers == 2:
        owns = [own, swap(own, 1)]
    else:
        groups = [list(range(g * sharers, (g + 1) * sharers)) for g in range(KV)]
        gathered = lax.all_gather(own, "seq", axis=0, axis_index_groups=groups)
        owns = [gathered[i] for i in range(sharers)]

    send_first, send_others = sends
    other_first = swap(send_first, 1)
    send_others, owns, other_query, close = lax.optimization_barrier((send_others, owns, other_query, close))
    other_others = swap(send_others, 1)
    state = begin([pieces[0], *close], owns, query, other_query)
    w_out, state = lax.optimization_barrier((w_out, state))
    mine_first, mine_others = half(w_out, chips, (True, first), (True, others))
    state, mine_first, mine_others = lax.optimization_barrier((state, mine_first, mine_others))
    state, sums = finish(far_parts, state)

    attention, *terms = merge(state, sums, swap(state, 1), swap(sums, 1), mine_first, other_first, rows)
    terms = dict(zip(first, terms))
    terms.update(zip(others, rest(attention, mine_others, other_others)))
    right = left = None
    for step in reversed(range(1, reach + 1)):
        term = terms[step]
        right = term if right is None else (right.astype(jnp.float32) + term).astype(jnp.bfloat16)
        right = around(right, 1)
        if step < reach:
            term = terms[chips - step]
            left = term if left is None else (left.astype(jnp.float32) + term).astype(jnp.bfloat16)
            left = around(left, -1)
    total = terms[0] + right.astype(jnp.float32)
    if left is not None:
        total += left.astype(jnp.float32)
    return total.astype(jnp.bfloat16)


def solution(mesh):
    return jax.shard_map(
        functools.partial(body, size=mesh.shape["seq"]),
        mesh=mesh,
        in_specs=(
            P("group", "seq"),
            P("seq"),
            P("seq", None),
            P("seq", None),
            P("seq", None),
            P("seq", None),
            P(None, ("group", "seq"), None),
        ),
        out_specs=P("group", "seq"),
        check_vma=False,
    )
```

```python
import functools
import math

import jax
import jax.numpy as jnp
from jax import lax
from jax.experimental import pallas as pl
from jax.experimental.pallas import tpu as pltpu
from jax.sharding import PartitionSpec as P

H = 64
KV = 8
DH = 128
EPS = 1e-05
PAD = 16
BLOCK = 512
MIB = 1 << 20
TRANS_B = (((1,), (1,)), ((), ()))


def in_vmem(count):
    return [pl.BlockSpec(memory_space=pltpu.VMEM)] * count


def anywhere(count):
    return [pl.BlockSpec(memory_space=pl.ANY)] * count


def cost(flops, moved):
    return pl.CostEstimate(flops=flops, bytes_accessed=moved, transcendentals=0)


def params(mib):
    return pltpu.CompilerParams(vmem_limit_bytes=mib * MIB)


def chip_at(place, chips):
    return jnp.where(place < chips // 2, 2 * place, 2 * (chips - 1 - place) + 1)


def place_of(chip, chips):
    return jnp.where(lax.rem(chip, 2) == 0, lax.div(chip, 2), chips - 1 - lax.div(chip, 2))


def here():
    device = lax.axis_index("seq")
    return lax.div(device, 2), lax.rem(device, 2)


def neighbour_chip(offset, chips):
    chip, _ = here()
    return chip_at(lax.rem(place_of(chip, chips) + offset + chips, chips), chips)


def pack_kernel(tokens, gain, block, near, sems):
    rows, width = tokens.shape
    copies = [
        pltpu.make_async_copy(gain, near, sems.at[0]),
        pltpu.make_async_copy(tokens, block.at[pl.ds(0, rows), :], sems.at[1]),
    ]
    for copy in copies:
        copy.start()
    copies[0].wait()
    wide = near[...].astype(jnp.float32).reshape(1, width)
    block[rows:, :] = jnp.broadcast_to(wide, (PAD, width)).astype(jnp.bfloat16)
    copies[1].wait()


def pack(tokens, gain):
    rows, width = tokens.shape
    return pl.pallas_call(
        pack_kernel,
        out_shape=pltpu.VMEM((rows + PAD, width), jnp.bfloat16),
        in_specs=anywhere(2),
        out_specs=in_vmem(1)[0],
        scratch_shapes=[pltpu.VMEM((width,), jnp.bfloat16), pltpu.SemaphoreType.DMA((2,))],
        name="pack",
    )(in_hbm(tokens), in_hbm(gain))


def cut_kernel(chips, cache, *pieces):
    chip, _ = here()
    for step, piece in enumerate(pieces):
        head = lax.div(lax.bitwise_xor(chip, step) * KV, chips)
        piece[...] = cache[:, :, pl.ds(pl.multiple_of(head * DH, DH), DH)]


def cut(cache, chips):
    shape = (2, cache.shape[1], DH)
    return pl.pallas_call(
        functools.partial(cut_kernel, chips),
        out_shape=[jax.ShapeDtypeStruct(shape, jnp.bfloat16)] * chips,
        in_specs=in_vmem(1),
        out_specs=in_vmem(chips),
        compiler_params=params(8),
        name="cut",
    )(cache)


def half_kernel(groups, chips, width, w_out, *refs):
    outs, sems = refs[:-1], refs[-1]
    _, core = here()
    copies = []
    for out, (mine, offsets) in zip(outs, groups):
        for number, offset in enumerate(offsets):
            column = 2 * neighbour_chip(offset, chips) + (core if mine else 1 - core)
            columns = pl.ds(pl.multiple_of(column * width, width), width)
            copy = pltpu.make_async_copy(w_out.at[:, columns], out.at[number], sems.at[len(copies)])
            copy.start()
            copies.append(copy)
    for copy in copies:
        copy.wait()


def in_hbm(value):
    return pltpu.with_memory_space_constraint(value, pltpu.HBM)


def half(w_out, chips, *groups):
    rows, columns = w_out.shape
    width = columns // (2 * chips)
    return pl.pallas_call(
        functools.partial(half_kernel, groups, chips, width),
        out_shape=[jax.ShapeDtypeStruct((len(offsets), rows, width), jnp.bfloat16) for _, offsets in groups],
        in_specs=anywhere(1),
        out_specs=in_vmem(len(groups)),
        scratch_shapes=[pltpu.SemaphoreType.DMA((sum(len(offsets) for _, offsets in groups),))],
        compiler_params=params(12),
        name="half",
    )(in_hbm(w_out))


def fetch_kernel(start, size, source, target, sem):
    copy = pltpu.make_async_copy(source.at[pl.ds(start, size), :], target, sem)
    copy.start()
    copy.wait()


def fetch(value, start, size):
    return pl.pallas_call(
        functools.partial(fetch_kernel, start, size),
        out_shape=pltpu.VMEM((size, value.shape[1]), jnp.bfloat16),
        in_specs=anywhere(1),
        out_specs=in_vmem(1)[0],
        scratch_shapes=[pltpu.SemaphoreType.DMA],
        compiler_params=params(8),
        cost_estimate=cost(0, 4 * size * value.shape[1]),
        name="fetch",
    )(in_hbm(value))


def project_kernel(offsets, chips, rows, *refs):
    count = len(offsets)
    blocks = refs[:count]
    w_first, w_second, w_key, w_value, query_ref, own_ref, held_own, own_sems = refs[count:]
    width = blocks[0].shape[1]
    side, middle = w_key.shape[0], w_first.shape[0]
    _, core = here()
    own_copies = [
        pltpu.make_async_copy(w_key, held_own.at[pl.ds(0, side), :], own_sems.at[0]),
        pltpu.make_async_copy(w_value, held_own.at[pl.ds(side, side), :], own_sems.at[1]),
    ]
    for copy in own_copies:
        copy.start()
    total = jnp.zeros((rows, 128), jnp.float32)
    for block in blocks:
        wide = block[:rows, :].astype(jnp.float32)
        square = wide * wide
        for lane in range(0, width, 128):
            total += square[:, lane : lane + 128]
    inverse = lax.rsqrt(jnp.sum(total, axis=1, keepdims=True) / (width * count) + EPS)
    first = jnp.zeros((rows, middle), jnp.float32)
    second = jnp.zeros((rows, middle), jnp.float32)
    own = jnp.zeros(own_ref.shape, jnp.float32)
    for copy in own_copies:
        copy.wait()
    for block, (offset, other) in zip(blocks, offsets):
        owner = 2 * neighbour_chip(offset, chips) + (1 - core if other else core)
        columns = pl.ds(pl.multiple_of(owner * width, width), width)
        gain = block[rows : rows + PAD, :].astype(jnp.float32)[0:1, :]
        wide = block[:rows, :].astype(jnp.float32)
        normed = (wide * inverse * gain).astype(jnp.bfloat16)
        own += lax.dot_general(normed, held_own[:, columns], TRANS_B, preferred_element_type=jnp.float32)
        first += lax.dot_general(normed, w_first[:, columns], TRANS_B, preferred_element_type=jnp.float32)
        second += lax.dot_general(normed, w_second[:, columns], TRANS_B, preferred_element_type=jnp.float32)
    query_ref[:, :middle] = first.astype(jnp.bfloat16)
    query_ref[:, middle:] = second.astype(jnp.bfloat16)
    own_ref[...] = own.astype(jnp.bfloat16)


def project(offsets, chips, blocks, w_first, w_second, w_key, w_value, rows):
    count = len(blocks)
    return pl.pallas_call(
        functools.partial(project_kernel, offsets, chips, rows),
        out_shape=(
            jax.ShapeDtypeStruct((rows, 2 * w_first.shape[0]), jnp.bfloat16),
            jax.ShapeDtypeStruct((rows, 2 * w_key.shape[0]), jnp.bfloat16),
        ),
        in_specs=in_vmem(count + 2) + anywhere(2),
        out_specs=tuple(in_vmem(2)),
        scratch_shapes=[
            pltpu.VMEM((2 * w_key.shape[0], w_key.shape[1]), jnp.bfloat16),
            pltpu.SemaphoreType.DMA((2,)),
        ],
        compiler_params=params(12),
        name="project",
    )(*blocks, w_first, w_second, in_hbm(w_key), in_hbm(w_value))


def weigh(query, caches, scores, top, total, numerator):
    scale = 1.0 / math.sqrt(DH)
    step = caches[0].shape[1]
    best = None
    for number, cache in enumerate(caches):
        part = lax.dot_general(query, cache[0], TRANS_B, preferred_element_type=jnp.float32)
        scores[:, number * step : (number + 1) * step] = part
        for lane in range(0, step, 128):
            piece = part[:, lane : lane + 128]
            best = piece if best is None else jnp.maximum(best, piece)
    before = top
    top = jnp.maximum(jnp.max(best, axis=1, keepdims=True) * scale, top)
    shrink = jnp.exp(before - top)
    total, numerator = total * shrink, numerator * shrink
    for number, cache in enumerate(caches):
        weights = jnp.exp(scores[:, number * step : (number + 1) * step] * scale - top)
        for lane in range(0, step, 128):
            total += weights[:, lane : lane + 128]
        numerator += jnp.dot(weights.astype(jnp.bfloat16), cache[1], preferred_element_type=jnp.float32)
    return top, total, numerator


def begin_kernel(count, parts, heads, *refs):
    caches, owns = refs[:count], refs[count : count + parts]
    mine, other, query_all, top_ref, total_ref, numerator_ref, scores = refs[count + parts :]
    rows = mine.shape[0]
    lines = heads * rows
    side = owns[0].shape[1] // 2
    _, core = here()
    own_parts = [own[...].astype(jnp.float32) for own in owns]
    if parts == 2:
        own_parts = [jnp.where(core == 0, own_parts[i], own_parts[1 - i]) for i in range(2)]
    own_key = jnp.concatenate([part[:, :side] for part in own_parts], axis=1)
    own_value = jnp.concatenate([part[:, side:] for part in own_parts], axis=1)
    for number, query_ref in enumerate((mine, other)):
        for head in range(heads):
            start = number * lines + head * rows
            query_all[start : start + rows, :] = query_ref[:, head * DH : (head + 1) * DH]
    lane = lax.broadcasted_iota(jnp.int32, (rows, 128), 1)
    for start in range(0, 2 * lines, rows):
        some = slice(start, start + rows)
        query = query_all[some, :]
        own = jnp.sum(query.astype(jnp.float32) * own_key, axis=1, keepdims=True) / math.sqrt(DH)
        mine_here = start < lines
        total = jnp.where(lane == 0, 1.0, 0.0) if mine_here else jnp.zeros((rows, 128), jnp.float32)
        numerator = own_value if mine_here else jnp.zeros((rows, DH), jnp.float32)
        top, total, numerator = weigh(query, caches, scores.at[some, :], own, total, numerator)
        top_ref[some, :] = jnp.broadcast_to(top, (rows, 128))
        total_ref[some, :] = total
        numerator_ref[some, :] = numerator


def begin(caches, owns, mine, other):
    count, rows = len(caches), mine.shape[0]
    heads = mine.shape[1] // DH
    lines = 2 * heads * rows
    positions = count * caches[0].shape[1]
    return pl.pallas_call(
        functools.partial(begin_kernel, count, len(owns), heads),
        out_shape=[jax.ShapeDtypeStruct((lines, DH), jnp.bfloat16)]
        + [jax.ShapeDtypeStruct((lines, 128), jnp.float32)] * 3,
        in_specs=in_vmem(count + len(owns) + 2),
        out_specs=in_vmem(4),
        scratch_shapes=[pltpu.VMEM((lines, positions), jnp.float32)],
        compiler_params=params(24),
        cost_estimate=cost(1, 1),
        name="begin",
    )(*caches, *owns, mine, other)


def finish_kernel(count, *refs):
    caches = refs[:count]
    query_all, top_ref, total_ref, numerator_ref, state_ref, sum_ref, scores = refs[count:]
    lines = query_all.shape[0]
    for start in range(0, lines, BLOCK):
        some = slice(start, start + BLOCK)
        top, total, numerator = weigh(
            query_all[some, :], caches, scores.at[some, :], top_ref[some, 0:1], total_ref[some, :], numerator_ref[some, :]
        )
        lane = lax.broadcasted_iota(jnp.int32, total.shape, 1)
        state_ref[some, :] = jnp.where(lane < 64, top, jnp.sum(total, axis=1, keepdims=True))
        sum_ref[some, :] = numerator


def finish(caches, state):
    count = len(caches)
    lines = state[0].shape[0]
    positions = count * caches[0].shape[1]
    return pl.pallas_call(
        functools.partial(finish_kernel, count),
        out_shape=[jax.ShapeDtypeStruct((lines, 128), jnp.float32)] * 2,
        in_specs=in_vmem(count + 4),
        out_specs=in_vmem(2),
        scratch_shapes=[pltpu.VMEM((lines, positions), jnp.float32)],
        compiler_params=params(24),
        name="finish",
    )(*caches, *state)


def output_term(attention, weights):
    return sum(
        jnp.dot(part, weight, preferred_element_type=jnp.float32) for part, weight in zip(attention, weights)
    )


def merge_kernel(rows, *refs):
    state, sums, far_state, far_sums, mine, other = refs[:6]
    attention_ref, outs = refs[6], refs[7:]
    lines = state.shape[0] // 2
    heads = lines // rows
    parts = []
    for number in range(2):
        near_lines = slice(number * lines, (number + 1) * lines)
        far_lines = slice((1 - number) * lines, (2 - number) * lines)
        top, far_top = state[near_lines, 0:1], far_state[far_lines, 0:1]
        peak = jnp.maximum(top, far_top)
        scale, far_scale = jnp.exp(top - peak), jnp.exp(far_top - peak)
        denominator = state[near_lines, 64:65] * scale + far_state[far_lines, 64:65] * far_scale
        numerator = sums[near_lines, :] * scale + far_sums[far_lines, :] * far_scale
        result = (numerator / denominator).astype(jnp.bfloat16)
        for head in range(heads):
            attention_ref[number, :, head * DH : (head + 1) * DH] = result[head * rows : (head + 1) * rows, :]
        parts.append(attention_ref[number])
    for number, out in enumerate(outs):
        out[...] = output_term(parts, (mine[number], other[number])).astype(out.dtype)


def merge(state, sums, far_state, far_sums, mine, other, rows):
    count, depth, width = mine.shape
    return pl.pallas_call(
        functools.partial(merge_kernel, rows),
        out_shape=[jax.ShapeDtypeStruct((2, rows, depth), jnp.bfloat16)]
        + [jax.ShapeDtypeStruct((rows, width), jnp.bfloat16)] * count,
        in_specs=in_vmem(6),
        out_specs=in_vmem(1 + count),
        compiler_params=params(16),
        name="merge",
    )(state, sums, far_state, far_sums, mine, other)


def rest_kernel(attention, mine, other, *outs):
    for number, out in enumerate(outs):
        out[...] = output_term((attention[0], attention[1]), (mine[number], other[number]))


def rest(attention, mine, other):
    count, _, width = mine.shape
    return pl.pallas_call(
        rest_kernel,
        out_shape=[jax.ShapeDtypeStruct((attention.shape[1], width), jnp.float32)] * count,
        in_specs=in_vmem(3),
        out_specs=in_vmem(count),
        compiler_params=params(12),
        name="rest",
    )(attention, mine, other)


def body(tokens, gain, w_query, w_key, w_value, w_out, prefix_cache, size):
    chips = size // 2
    outer = chips // 2
    cycle = [2 * a for a in range(outer)] + [2 * a + 1 for a in reversed(range(outer))]

    def around(value, step):
        pairs = [
            (2 * cycle[p] + k, 2 * cycle[(p + step) % chips] + k) for p in range(chips) for k in (0, 1)
        ]
        return lax.ppermute(value, "seq", pairs)

    def swap(value, bits):
        return lax.ppermute(value, "seq", [(i, i ^ bits) for i in range(size)])

    rows = tokens.shape[0]

    block = pack(tokens, gain)
    blocks, offsets = [], []

    def take(value, offset):
        blocks.extend([value, swap(value, 1)])
        offsets.extend([(offset, False), (offset, True)])

    right = left = block
    reach = chips // 2
    take(block, 0)
    middle = w_query.shape[0] // 2
    weights = []
    first = tuple([reach] + ([chips - reach + 1] if reach > 1 else []))
    others = tuple(offset for offset in range(chips) if offset not in first)
    for step in range(1, reach + 1):
        if step > 1:
            right, weights = lax.optimization_barrier((right, weights))
        if step <= 2:
            w_query, right = lax.optimization_barrier((w_query, right))
            weights = [*weights, fetch(w_query, (step - 1) * middle, middle)]
        right = around(right, 1)
        if step == 1:
            prefix_cache, right = lax.optimization_barrier((prefix_cache, right))
            pieces = cut(prefix_cache, chips)
        if step == min(2, reach):
            pieces, right = lax.optimization_barrier((pieces, right))
        if step == max(reach - 1, 1):
            pieces, right = lax.optimization_barrier((pieces, right))
        take(right, -step)
        if step < reach:
            left = around(left, -1)
            take(left, step)

    soon = (chips - reach) // 2
    sooner = [*range(reach, reach + soon), *range(1, reach)]
    later = [step for step in range(1, chips) if step not in sooner]
    close = [swap(pieces[step], 2 * step) for step in sooner]
    pieces, close = lax.optimization_barrier((pieces, close))
    far_parts = [swap(pieces[step], 2 * step) for step in later]
    query, own = project(tuple(offsets), chips, blocks, *weights, w_key, w_value, rows)

    w_out, query = lax.optimization_barrier((w_out, query))
    sends = half(w_out, chips, (False, first), (False, others))
    query, own, sends = lax.optimization_barrier((query, own, sends))

    sharers = size // KV
    other_query = swap(query, 1)
    if sharers == 2:
        owns = [own, swap(own, 1)]
    else:
        groups = [list(range(g * sharers, (g + 1) * sharers)) for g in range(KV)]
        gathered = lax.all_gather(own, "seq", axis=0, axis_index_groups=groups)
        owns = [gathered[i] for i in range(sharers)]

    send_first, send_others = sends
    other_first = swap(send_first, 1)
    send_others, owns, other_query, close = lax.optimization_barrier((send_others, owns, other_query, close))
    other_others = swap(send_others, 1)
    state = begin([pieces[0], *close], owns, query, other_query)
    w_out, state = lax.optimization_barrier((w_out, state))
    mine_first, mine_others = half(w_out, chips, (True, first), (True, others))
    state, mine_first, mine_others = lax.optimization_barrier((state, mine_first, mine_others))
    state, sums = finish(far_parts, state)

    attention, *terms = merge(state, sums, swap(state, 1), swap(sums, 1), mine_first, other_first, rows)
    terms = dict(zip(first, terms))
    terms.update(zip(others, rest(attention, mine_others, other_others)))
    right = left = None
    for step in reversed(range(1, reach + 1)):
        term = terms[step]
        right = term if right is None else (right.astype(jnp.float32) + term).astype(jnp.bfloat16)
        right = around(right, 1)
        if step < reach:
            term = terms[chips - step]
            left = term if left is None else (left.astype(jnp.float32) + term).astype(jnp.bfloat16)
            left = around(left, -1)
    total = terms[0] + right.astype(jnp.float32)
    if left is not None:
        total += left.astype(jnp.float32)
    return total.astype(jnp.bfloat16)


def solution(mesh):
    return jax.shard_map(
        functools.partial(body, size=mesh.shape["seq"]),
        mesh=mesh,
        in_specs=(
            P("group", "seq"),
            P("seq"),
            P("seq", None),
            P("seq", None),
            P("seq", None),
            P("seq", None),
            P(None, ("group", "seq"), None),
        ),
        out_specs=P("group", "seq"),
        check_vma=False,
    )
```

```python
import functools
import math

import jax
import jax.numpy as jnp
from jax import lax
from jax.experimental import pallas as pl
from jax.experimental.pallas import tpu as pltpu
from jax.sharding import PartitionSpec as P

H = 64
KV = 8
DH = 128
EPS = 1e-05
PAD = 16
BLOCK = 512
MIB = 1 << 20
TRANS_B = (((1,), (1,)), ((), ()))


def in_vmem(count):
    return [pl.BlockSpec(memory_space=pltpu.VMEM)] * count


def anywhere(count):
    return [pl.BlockSpec(memory_space=pl.ANY)] * count


def cost(flops, moved):
    return pl.CostEstimate(flops=flops, bytes_accessed=moved, transcendentals=0)


def params(mib):
    return pltpu.CompilerParams(vmem_limit_bytes=mib * MIB)


def chip_at(place, chips):
    return jnp.where(place < chips // 2, 2 * place, 2 * (chips - 1 - place) + 1)


def place_of(chip, chips):
    return jnp.where(lax.rem(chip, 2) == 0, lax.div(chip, 2), chips - 1 - lax.div(chip, 2))


def here():
    device = lax.axis_index("seq")
    return lax.div(device, 2), lax.rem(device, 2)


def neighbour_chip(offset, chips):
    chip, _ = here()
    return chip_at(lax.rem(place_of(chip, chips) + offset + chips, chips), chips)


def pack_kernel(tokens, gain, block, near, sems):
    rows, width = tokens.shape
    copies = [
        pltpu.make_async_copy(gain, near, sems.at[0]),
        pltpu.make_async_copy(tokens, block.at[pl.ds(0, rows), :], sems.at[1]),
    ]
    for copy in copies:
        copy.start()
    copies[0].wait()
    wide = near[...].astype(jnp.float32).reshape(1, width)
    block[rows:, :] = jnp.broadcast_to(wide, (PAD, width)).astype(jnp.bfloat16)
    copies[1].wait()


def pack(tokens, gain):
    rows, width = tokens.shape
    return pl.pallas_call(
        pack_kernel,
        out_shape=pltpu.VMEM((rows + PAD, width), jnp.bfloat16),
        in_specs=anywhere(2),
        out_specs=in_vmem(1)[0],
        scratch_shapes=[pltpu.VMEM((width,), jnp.bfloat16), pltpu.SemaphoreType.DMA((2,))],
        name="pack",
    )(in_hbm(tokens), in_hbm(gain))


def cut_kernel(chips, cache, *pieces):
    chip, _ = here()
    for step, piece in enumerate(pieces):
        head = lax.div(lax.bitwise_xor(chip, step) * KV, chips)
        piece[...] = cache[:, :, pl.ds(pl.multiple_of(head * DH, DH), DH)]


def cut(cache, chips):
    shape = (2, cache.shape[1], DH)
    return pl.pallas_call(
        functools.partial(cut_kernel, chips),
        out_shape=[jax.ShapeDtypeStruct(shape, jnp.bfloat16)] * chips,
        in_specs=in_vmem(1),
        out_specs=in_vmem(chips),
        compiler_params=params(8),
        name="cut",
    )(cache)


def half_kernel(groups, chips, width, w_out, *refs):
    outs, sems = refs[:-1], refs[-1]
    _, core = here()
    copies = []
    for out, (mine, offsets) in zip(outs, groups):
        for number, offset in enumerate(offsets):
            column = 2 * neighbour_chip(offset, chips) + (core if mine else 1 - core)
            columns = pl.ds(pl.multiple_of(column * width, width), width)
            copy = pltpu.make_async_copy(w_out.at[:, columns], out.at[number], sems.at[len(copies)])
            copy.start()
            copies.append(copy)
    for copy in copies:
        copy.wait()


def in_hbm(value):
    return pltpu.with_memory_space_constraint(value, pltpu.HBM)


def half(w_out, chips, *groups):
    rows, columns = w_out.shape
    width = columns // (2 * chips)
    return pl.pallas_call(
        functools.partial(half_kernel, groups, chips, width),
        out_shape=[jax.ShapeDtypeStruct((len(offsets), rows, width), jnp.bfloat16) for _, offsets in groups],
        in_specs=anywhere(1),
        out_specs=in_vmem(len(groups)),
        scratch_shapes=[pltpu.SemaphoreType.DMA((sum(len(offsets) for _, offsets in groups),))],
        compiler_params=params(12),
        name="half",
    )(in_hbm(w_out))


def fetch_kernel(start, size, source, target, sem):
    copy = pltpu.make_async_copy(source.at[pl.ds(start, size), :], target, sem)
    copy.start()
    copy.wait()


def fetch(value, start, size):
    return pl.pallas_call(
        functools.partial(fetch_kernel, start, size),
        out_shape=pltpu.VMEM((size, value.shape[1]), jnp.bfloat16),
        in_specs=anywhere(1),
        out_specs=in_vmem(1)[0],
        scratch_shapes=[pltpu.SemaphoreType.DMA],
        compiler_params=params(8),
        cost_estimate=cost(0, 4 * size * value.shape[1]),
        name="fetch",
    )(in_hbm(value))


def project_kernel(offsets, chips, rows, *refs):
    count = len(offsets)
    blocks = refs[:count]
    w_first, w_second, w_key, w_value, query_ref, own_ref, held_own, own_sems = refs[count:]
    width = blocks[0].shape[1]
    side, middle = w_key.shape[0], w_first.shape[0]
    _, core = here()
    own_copies = [
        pltpu.make_async_copy(w_key, held_own.at[pl.ds(0, side), :], own_sems.at[0]),
        pltpu.make_async_copy(w_value, held_own.at[pl.ds(side, side), :], own_sems.at[1]),
    ]
    for copy in own_copies:
        copy.start()
    total = jnp.zeros((rows, 128), jnp.float32)
    for block in blocks:
        wide = block[:rows, :].astype(jnp.float32)
        square = wide * wide
        for lane in range(0, width, 128):
            total += square[:, lane : lane + 128]
    inverse = lax.rsqrt(jnp.sum(total, axis=1, keepdims=True) / (width * count) + EPS)
    first = jnp.zeros((rows, middle), jnp.float32)
    second = jnp.zeros((rows, middle), jnp.float32)
    own = jnp.zeros(own_ref.shape, jnp.float32)
    for copy in own_copies:
        copy.wait()
    for block, (offset, other) in zip(blocks, offsets):
        owner = 2 * neighbour_chip(offset, chips) + (1 - core if other else core)
        columns = pl.ds(pl.multiple_of(owner * width, width), width)
        gain = block[rows : rows + PAD, :].astype(jnp.float32)[0:1, :]
        wide = block[:rows, :].astype(jnp.float32)
        normed = (wide * inverse * gain).astype(jnp.bfloat16)
        own += lax.dot_general(normed, held_own[:, columns], TRANS_B, preferred_element_type=jnp.float32)
        first += lax.dot_general(normed, w_first[:, columns], TRANS_B, preferred_element_type=jnp.float32)
        second += lax.dot_general(normed, w_second[:, columns], TRANS_B, preferred_element_type=jnp.float32)
    query_ref[:, :middle] = first.astype(jnp.bfloat16)
    query_ref[:, middle:] = second.astype(jnp.bfloat16)
    own_ref[...] = own.astype(jnp.bfloat16)


def project(offsets, chips, blocks, w_first, w_second, w_key, w_value, rows):
    count = len(blocks)
    return pl.pallas_call(
        functools.partial(project_kernel, offsets, chips, rows),
        out_shape=(
            jax.ShapeDtypeStruct((rows, 2 * w_first.shape[0]), jnp.bfloat16),
            jax.ShapeDtypeStruct((rows, 2 * w_key.shape[0]), jnp.bfloat16),
        ),
        in_specs=in_vmem(count + 2) + anywhere(2),
        out_specs=tuple(in_vmem(2)),
        scratch_shapes=[
            pltpu.VMEM((2 * w_key.shape[0], w_key.shape[1]), jnp.bfloat16),
            pltpu.SemaphoreType.DMA((2,)),
        ],
        compiler_params=params(12),
        name="project",
    )(*blocks, w_first, w_second, in_hbm(w_key), in_hbm(w_value))


def weigh(query, caches, scores, top, total, numerator):
    scale = 1.0 / math.sqrt(DH)
    step = caches[0].shape[1]
    best = None
    for number, cache in enumerate(caches):
        part = lax.dot_general(query, cache[0], TRANS_B, preferred_element_type=jnp.float32)
        scores[:, number * step : (number + 1) * step] = part
        for lane in range(0, step, 128):
            piece = part[:, lane : lane + 128]
            best = piece if best is None else jnp.maximum(best, piece)
    before = top
    top = jnp.maximum(jnp.max(best, axis=1, keepdims=True) * scale, top)
    shrink = jnp.exp(before - top)
    total, numerator = total * shrink, numerator * shrink
    for number, cache in enumerate(caches):
        weights = jnp.exp(scores[:, number * step : (number + 1) * step] * scale - top)
        for lane in range(0, step, 128):
            total += weights[:, lane : lane + 128]
        numerator += jnp.dot(weights.astype(jnp.bfloat16), cache[1], preferred_element_type=jnp.float32)
    return top, total, numerator


def begin_kernel(count, parts, heads, *refs):
    caches, owns = refs[:count], refs[count : count + parts]
    mine, other, query_all, top_ref, total_ref, numerator_ref, scores = refs[count + parts :]
    rows = mine.shape[0]
    lines = heads * rows
    side = owns[0].shape[1] // 2
    _, core = here()
    own_parts = [own[...].astype(jnp.float32) for own in owns]
    if parts == 2:
        own_parts = [jnp.where(core == 0, own_parts[i], own_parts[1 - i]) for i in range(2)]
    own_key = jnp.concatenate([part[:, :side] for part in own_parts], axis=1)
    own_value = jnp.concatenate([part[:, side:] for part in own_parts], axis=1)
    for number, query_ref in enumerate((mine, other)):
        for head in range(heads):
            start = number * lines + head * rows
            query_all[start : start + rows, :] = query_ref[:, head * DH : (head + 1) * DH]
    lane = lax.broadcasted_iota(jnp.int32, (rows, 128), 1)
    for start in range(0, 2 * lines, rows):
        some = slice(start, start + rows)
        query = query_all[some, :]
        own = jnp.sum(query.astype(jnp.float32) * own_key, axis=1, keepdims=True) / math.sqrt(DH)
        mine_here = start < lines
        total = jnp.where(lane == 0, 1.0, 0.0) if mine_here else jnp.zeros((rows, 128), jnp.float32)
        numerator = own_value if mine_here else jnp.zeros((rows, DH), jnp.float32)
        top, total, numerator = weigh(query, caches, scores.at[some, :], own, total, numerator)
        top_ref[some, :] = jnp.broadcast_to(top, (rows, 128))
        total_ref[some, :] = total
        numerator_ref[some, :] = numerator


def begin(caches, owns, mine, other):
    count, rows = len(caches), mine.shape[0]
    heads = mine.shape[1] // DH
    lines = 2 * heads * rows
    positions = count * caches[0].shape[1]
    return pl.pallas_call(
        functools.partial(begin_kernel, count, len(owns), heads),
        out_shape=[jax.ShapeDtypeStruct((lines, DH), jnp.bfloat16)]
        + [jax.ShapeDtypeStruct((lines, 128), jnp.float32)] * 3,
        in_specs=in_vmem(count + len(owns) + 2),
        out_specs=in_vmem(4),
        scratch_shapes=[pltpu.VMEM((lines, positions), jnp.float32)],
        compiler_params=params(24),
        cost_estimate=cost(1, 1),
        name="begin",
    )(*caches, *owns, mine, other)


def finish_kernel(count, *refs):
    caches = refs[:count]
    query_all, top_ref, total_ref, numerator_ref, state_ref, sum_ref, scores = refs[count:]
    lines = query_all.shape[0]
    for start in range(0, lines, BLOCK):
        some = slice(start, start + BLOCK)
        top, total, numerator = weigh(
            query_all[some, :], caches, scores.at[some, :], top_ref[some, 0:1], total_ref[some, :], numerator_ref[some, :]
        )
        lane = lax.broadcasted_iota(jnp.int32, total.shape, 1)
        state_ref[some, :] = jnp.where(lane < 64, top, jnp.sum(total, axis=1, keepdims=True))
        sum_ref[some, :] = numerator


def finish(caches, state):
    count = len(caches)
    lines = state[0].shape[0]
    positions = count * caches[0].shape[1]
    return pl.pallas_call(
        functools.partial(finish_kernel, count),
        out_shape=[jax.ShapeDtypeStruct((lines, 128), jnp.float32)] * 2,
        in_specs=in_vmem(count + 4),
        out_specs=in_vmem(2),
        scratch_shapes=[pltpu.VMEM((lines, positions), jnp.float32)],
        compiler_params=params(24),
        name="finish",
    )(*caches, *state)


def output_term(attention, weights):
    return sum(
        jnp.dot(part, weight, preferred_element_type=jnp.float32) for part, weight in zip(attention, weights)
    )


def merge_kernel(rows, *refs):
    state, sums, far_state, far_sums, mine, other = refs[:6]
    attention_ref, outs = refs[6], refs[7:]
    lines = state.shape[0] // 2
    heads = lines // rows
    parts = []
    for number in range(2):
        near_lines = slice(number * lines, (number + 1) * lines)
        far_lines = slice((1 - number) * lines, (2 - number) * lines)
        top, far_top = state[near_lines, 0:1], far_state[far_lines, 0:1]
        peak = jnp.maximum(top, far_top)
        scale, far_scale = jnp.exp(top - peak), jnp.exp(far_top - peak)
        denominator = state[near_lines, 64:65] * scale + far_state[far_lines, 64:65] * far_scale
        numerator = sums[near_lines, :] * scale + far_sums[far_lines, :] * far_scale
        result = (numerator * (1.0 / denominator)).astype(jnp.bfloat16)
        for head in range(heads):
            attention_ref[number, :, head * DH : (head + 1) * DH] = result[head * rows : (head + 1) * rows, :]
        parts.append(attention_ref[number])
    for number, out in enumerate(outs):
        out[...] = output_term(parts, (mine[number], other[number])).astype(out.dtype)


def merge(state, sums, far_state, far_sums, mine, other, rows):
    count, depth, width = mine.shape
    return pl.pallas_call(
        functools.partial(merge_kernel, rows),
        out_shape=[jax.ShapeDtypeStruct((2, rows, depth), jnp.bfloat16)]
        + [jax.ShapeDtypeStruct((rows, width), jnp.bfloat16)] * count,
        in_specs=in_vmem(6),
        out_specs=in_vmem(1 + count),
        compiler_params=params(16),
        name="merge",
    )(state, sums, far_state, far_sums, mine, other)


def rest_kernel(attention, mine, other, *outs):
    for number, out in enumerate(outs):
        out[...] = output_term((attention[0], attention[1]), (mine[number], other[number]))


def rest(attention, mine, other):
    count, _, width = mine.shape
    return pl.pallas_call(
        rest_kernel,
        out_shape=[jax.ShapeDtypeStruct((attention.shape[1], width), jnp.float32)] * count,
        in_specs=in_vmem(3),
        out_specs=in_vmem(count),
        compiler_params=params(12),
        name="rest",
    )(attention, mine, other)


def body(tokens, gain, w_query, w_key, w_value, w_out, prefix_cache, size):
    chips = size // 2
    outer = chips // 2
    cycle = [2 * a for a in range(outer)] + [2 * a + 1 for a in reversed(range(outer))]

    def around(value, step):
        pairs = [
            (2 * cycle[p] + k, 2 * cycle[(p + step) % chips] + k) for p in range(chips) for k in (0, 1)
        ]
        return lax.ppermute(value, "seq", pairs)

    def swap(value, bits):
        return lax.ppermute(value, "seq", [(i, i ^ bits) for i in range(size)])

    rows = tokens.shape[0]

    block = pack(tokens, gain)
    blocks, offsets = [], []

    def take(value, offset):
        blocks.extend([value, swap(value, 1)])
        offsets.extend([(offset, False), (offset, True)])

    right = left = block
    reach = chips // 2
    take(block, 0)
    middle = w_query.shape[0] // 2
    weights = []
    first = tuple([reach] + ([chips - reach + 1] if reach > 1 else []))
    others = tuple(offset for offset in range(chips) if offset not in first)
    for step in range(1, reach + 1):
        if step > 1:
            right, weights = lax.optimization_barrier((right, weights))
        if step <= 2:
            w_query, right = lax.optimization_barrier((w_query, right))
            weights = [*weights, fetch(w_query, (step - 1) * middle, middle)]
        right = around(right, 1)
        if step == 1:
            prefix_cache, right = lax.optimization_barrier((prefix_cache, right))
            pieces = cut(prefix_cache, chips)
        if step == min(2, reach):
            pieces, right = lax.optimization_barrier((pieces, right))
        if step == max(reach - 1, 1):
            pieces, right = lax.optimization_barrier((pieces, right))
        take(right, -step)
        if step < reach:
            left = around(left, -1)
            take(left, step)

    soon = (chips - reach) // 2
    sooner = [*range(reach, reach + soon), *reversed(range(1, reach))]
    later = [*reversed(range(reach + soon, chips))]
    close = [swap(pieces[step], 2 * step) for step in sooner]
    pieces, close = lax.optimization_barrier((pieces, close))
    far_parts = [swap(pieces[step], 2 * step) for step in later]
    query, own = project(tuple(offsets), chips, blocks, *weights, w_key, w_value, rows)

    w_out, query = lax.optimization_barrier((w_out, query))
    sends = half(w_out, chips, (False, first), (False, others))
    query, own, sends = lax.optimization_barrier((query, own, sends))

    sharers = size // KV
    other_query = swap(query, 1)
    if sharers == 2:
        owns = [own, swap(own, 1)]
    else:
        groups = [list(range(g * sharers, (g + 1) * sharers)) for g in range(KV)]
        gathered = lax.all_gather(own, "seq", axis=0, axis_index_groups=groups)
        owns = [gathered[i] for i in range(sharers)]

    send_first, send_others = sends
    other_first = swap(send_first, 1)
    send_others, owns, other_query, close = lax.optimization_barrier((send_others, owns, other_query, close))
    other_others = swap(send_others, 1)
    state = begin([pieces[0], *close], owns, query, other_query)
    w_out, state = lax.optimization_barrier((w_out, state))
    mine_first, mine_others = half(w_out, chips, (True, first), (True, others))
    state, mine_first, mine_others = lax.optimization_barrier((state, mine_first, mine_others))
    state, sums = finish(far_parts, state)

    attention, *terms = merge(state, sums, swap(state, 1), swap(sums, 1), mine_first, other_first, rows)
    terms = dict(zip(first, terms))
    terms.update(zip(others, rest(attention, mine_others, other_others)))
    right = left = None
    for step in reversed(range(1, reach + 1)):
        term = terms[step]
        right = term if right is None else (right.astype(jnp.float32) + term).astype(jnp.bfloat16)
        right = around(right, 1)
        if step < reach:
            term = terms[chips - step]
            left = term if left is None else (left.astype(jnp.float32) + term).astype(jnp.bfloat16)
            left = around(left, -1)
    total = terms[0] + right.astype(jnp.float32)
    if left is not None:
        total += left.astype(jnp.float32)
    return total.astype(jnp.bfloat16)


def solution(mesh):
    return jax.shard_map(
        functools.partial(body, size=mesh.shape["seq"]),
        mesh=mesh,
        in_specs=(
            P("group", "seq"),
            P("seq"),
            P("seq", None),
            P("seq", None),
            P("seq", None),
            P("seq", None),
            P(None, ("group", "seq"), None),
        ),
        out_specs=P("group", "seq"),
        check_vma=False,
    )
```

```python
import functools
import math

import jax
import jax.numpy as jnp
from jax import lax
from jax.experimental import pallas as pl
from jax.experimental.pallas import tpu as pltpu
from jax.sharding import PartitionSpec as P

H = 64
KV = 8
DH = 128
EPS = 1e-05
PAD = 16
MIB = 1 << 20
TRANS_B = (((1,), (1,)), ((), ()))


def in_vmem(count):
    return [pl.BlockSpec(memory_space=pltpu.VMEM)] * count


def anywhere(count):
    return [pl.BlockSpec(memory_space=pl.ANY)] * count


def cost(flops, moved):
    return pl.CostEstimate(flops=flops, bytes_accessed=moved, transcendentals=0)


def params(mib):
    return pltpu.CompilerParams(vmem_limit_bytes=mib * MIB)


def chip_at(place, chips):
    return jnp.where(place < chips // 2, 2 * place, 2 * (chips - 1 - place) + 1)


def place_of(chip, chips):
    return jnp.where(lax.rem(chip, 2) == 0, lax.div(chip, 2), chips - 1 - lax.div(chip, 2))


def here():
    device = lax.axis_index("seq")
    return lax.div(device, 2), lax.rem(device, 2)


def neighbour_chip(offset, chips):
    chip, _ = here()
    return chip_at(lax.rem(place_of(chip, chips) + offset + chips, chips), chips)


def pack_kernel(tokens, gain, block, near, sems):
    rows, width = tokens.shape
    copies = [
        pltpu.make_async_copy(gain, near, sems.at[0]),
        pltpu.make_async_copy(tokens, block.at[pl.ds(0, rows), :], sems.at[1]),
    ]
    for copy in copies:
        copy.start()
    copies[0].wait()
    wide = near[...].astype(jnp.float32).reshape(1, width)
    block[rows:, :] = jnp.broadcast_to(wide, (PAD, width)).astype(jnp.bfloat16)
    copies[1].wait()


def pack(tokens, gain):
    rows, width = tokens.shape
    return pl.pallas_call(
        pack_kernel,
        out_shape=pltpu.VMEM((rows + PAD, width), jnp.bfloat16),
        in_specs=anywhere(2),
        out_specs=in_vmem(1)[0],
        scratch_shapes=[pltpu.VMEM((width,), jnp.bfloat16), pltpu.SemaphoreType.DMA((2,))],
        name="pack",
    )(in_hbm(tokens), in_hbm(gain))


def cut_kernel(chips, cache, *pieces):
    chip, _ = here()
    for step, piece in enumerate(pieces):
        head = lax.div(lax.bitwise_xor(chip, step) * KV, chips)
        piece[...] = cache[:, :, pl.ds(pl.multiple_of(head * DH, DH), DH)]


def cut(cache, chips):
    shape = (2, cache.shape[1], DH)
    return pl.pallas_call(
        functools.partial(cut_kernel, chips),
        out_shape=[jax.ShapeDtypeStruct(shape, jnp.bfloat16)] * chips,
        in_specs=in_vmem(1),
        out_specs=in_vmem(chips),
        compiler_params=params(8),
        name="cut",
    )(cache)


def half_kernel(groups, chips, width, w_out, *refs):
    outs, sems = refs[:-1], refs[-1]
    _, core = here()
    copies = []
    for out, (mine, offsets) in zip(outs, groups):
        for number, offset in enumerate(offsets):
            column = 2 * neighbour_chip(offset, chips) + (core if mine else 1 - core)
            columns = pl.ds(pl.multiple_of(column * width, width), width)
            copy = pltpu.make_async_copy(w_out.at[:, columns], out.at[number], sems.at[len(copies)])
            copy.start()
            copies.append(copy)
    for copy in copies:
        copy.wait()


def in_hbm(value):
    return pltpu.with_memory_space_constraint(value, pltpu.HBM)


def half(w_out, chips, *groups):
    rows, columns = w_out.shape
    width = columns // (2 * chips)
    return pl.pallas_call(
        functools.partial(half_kernel, groups, chips, width),
        out_shape=[jax.ShapeDtypeStruct((len(offsets), rows, width), jnp.bfloat16) for _, offsets in groups],
        in_specs=anywhere(1),
        out_specs=in_vmem(len(groups)),
        scratch_shapes=[pltpu.SemaphoreType.DMA((sum(len(offsets) for _, offsets in groups),))],
        compiler_params=params(12),
        name="half",
    )(in_hbm(w_out))


def fetch_kernel(start, size, source, target, sem):
    copy = pltpu.make_async_copy(source.at[pl.ds(start, size), :], target, sem)
    copy.start()
    copy.wait()


def fetch(value, start, size):
    return pl.pallas_call(
        functools.partial(fetch_kernel, start, size),
        out_shape=pltpu.VMEM((size, value.shape[1]), jnp.bfloat16),
        in_specs=anywhere(1),
        out_specs=in_vmem(1)[0],
        scratch_shapes=[pltpu.SemaphoreType.DMA],
        compiler_params=params(8),
        cost_estimate=cost(0, 4 * size * value.shape[1]),
        name="fetch",
    )(in_hbm(value))


def project_kernel(offsets, chips, rows, *refs):
    count = len(offsets)
    blocks = refs[:count]
    w_first, w_second, w_key, w_value, query_ref, own_ref, held_own, own_sems = refs[count:]
    width = blocks[0].shape[1]
    side, middle = w_key.shape[0], w_first.shape[0]
    _, core = here()
    own_copies = [
        pltpu.make_async_copy(w_key, held_own.at[pl.ds(0, side), :], own_sems.at[0]),
        pltpu.make_async_copy(w_value, held_own.at[pl.ds(side, side), :], own_sems.at[1]),
    ]
    for copy in own_copies:
        copy.start()
    total = jnp.zeros((rows, 128), jnp.float32)
    for block in blocks:
        wide = block[:rows, :].astype(jnp.float32)
        square = wide * wide
        for lane in range(0, width, 128):
            total += square[:, lane : lane + 128]
    inverse = lax.rsqrt(jnp.sum(total, axis=1, keepdims=True) / (width * count) + EPS)
    first = jnp.zeros((rows, middle), jnp.float32)
    second = jnp.zeros((rows, middle), jnp.float32)
    own = jnp.zeros(own_ref.shape, jnp.float32)
    for copy in own_copies:
        copy.wait()
    for block, (offset, other) in zip(blocks, offsets):
        owner = 2 * neighbour_chip(offset, chips) + (1 - core if other else core)
        columns = pl.ds(pl.multiple_of(owner * width, width), width)
        gain = block[rows : rows + PAD, :].astype(jnp.float32)[0:1, :]
        wide = block[:rows, :].astype(jnp.float32)
        normed = (wide * inverse * gain).astype(jnp.bfloat16)
        own += lax.dot_general(normed, held_own[:, columns], TRANS_B, preferred_element_type=jnp.float32)
        first += lax.dot_general(normed, w_first[:, columns], TRANS_B, preferred_element_type=jnp.float32)
        second += lax.dot_general(normed, w_second[:, columns], TRANS_B, preferred_element_type=jnp.float32)
    query_ref[:, :middle] = first.astype(jnp.bfloat16)
    query_ref[:, middle:] = second.astype(jnp.bfloat16)
    own_ref[...] = own.astype(jnp.bfloat16)


def project(offsets, chips, blocks, w_first, w_second, w_key, w_value, rows):
    count = len(blocks)
    return pl.pallas_call(
        functools.partial(project_kernel, offsets, chips, rows),
        out_shape=(
            jax.ShapeDtypeStruct((rows, 2 * w_first.shape[0]), jnp.bfloat16),
            jax.ShapeDtypeStruct((rows, 2 * w_key.shape[0]), jnp.bfloat16),
        ),
        in_specs=in_vmem(count + 2) + anywhere(2),
        out_specs=tuple(in_vmem(2)),
        scratch_shapes=[
            pltpu.VMEM((2 * w_key.shape[0], w_key.shape[1]), jnp.bfloat16),
            pltpu.SemaphoreType.DMA((2,)),
        ],
        compiler_params=params(12),
        name="project",
    )(*blocks, w_first, w_second, in_hbm(w_key), in_hbm(w_value))


def weigh(query, caches, scores, top, total, numerator):
    scale = 1.0 / math.sqrt(DH)
    step = caches[0].shape[1]
    best = None
    for number, cache in enumerate(caches):
        part = lax.dot_general(query, cache[0], TRANS_B, preferred_element_type=jnp.float32)
        scores[:, number * step : (number + 1) * step] = part
        for lane in range(0, step, 128):
            piece = part[:, lane : lane + 128]
            best = piece if best is None else jnp.maximum(best, piece)
    before = top
    top = jnp.maximum(jnp.max(best, axis=1, keepdims=True) * scale, top)
    shrink = jnp.exp(before - top)
    total, numerator = total * shrink, numerator * shrink
    for number, cache in enumerate(caches):
        weights = jnp.exp(scores[:, number * step : (number + 1) * step] * scale - top)
        for lane in range(0, step, 128):
            total += weights[:, lane : lane + 128]
        numerator += jnp.dot(weights.astype(jnp.bfloat16), cache[1], preferred_element_type=jnp.float32)
    return top, total, numerator


def begin_kernel(count, parts, heads, *refs):
    caches, owns = refs[:count], refs[count : count + parts]
    mine, other, query_all, top_ref, total_ref, numerator_ref, scores = refs[count + parts :]
    rows = mine.shape[0]
    lines = heads * rows
    side = owns[0].shape[1] // 2
    _, core = here()
    own_parts = [own[...].astype(jnp.float32) for own in owns]
    if parts == 2:
        own_parts = [jnp.where(core == 0, own_parts[i], own_parts[1 - i]) for i in range(2)]
    own_key = jnp.concatenate([part[:, :side] for part in own_parts], axis=1)
    own_value = jnp.concatenate([part[:, side:] for part in own_parts], axis=1)
    for number, query_ref in enumerate((mine, other)):
        for head in range(heads):
            start = number * lines + head * rows
            query_all[start : start + rows, :] = query_ref[:, head * DH : (head + 1) * DH]
    lane = lax.broadcasted_iota(jnp.int32, (rows, 128), 1)
    for start in range(0, 2 * lines, rows):
        some = slice(start, start + rows)
        query = query_all[some, :]
        own = jnp.sum(query.astype(jnp.float32) * own_key, axis=1, keepdims=True) / math.sqrt(DH)
        mine_here = start < lines
        total = jnp.where(lane == 0, 1.0, 0.0) if mine_here else jnp.zeros((rows, 128), jnp.float32)
        numerator = own_value if mine_here else jnp.zeros((rows, DH), jnp.float32)
        top, total, numerator = weigh(query, caches, scores.at[some, :], own, total, numerator)
        top_ref[some, :] = jnp.broadcast_to(top, (rows, 128))
        total_ref[some, :] = total
        numerator_ref[some, :] = numerator


def begin(caches, owns, mine, other):
    count, rows = len(caches), mine.shape[0]
    heads = mine.shape[1] // DH
    lines = 2 * heads * rows
    positions = count * caches[0].shape[1]
    return pl.pallas_call(
        functools.partial(begin_kernel, count, len(owns), heads),
        out_shape=[jax.ShapeDtypeStruct((lines, DH), jnp.bfloat16)]
        + [jax.ShapeDtypeStruct((lines, 128), jnp.float32)] * 3,
        in_specs=in_vmem(count + len(owns) + 2),
        out_specs=in_vmem(4),
        scratch_shapes=[pltpu.VMEM((lines, positions), jnp.float32)],
        compiler_params=params(24),
        cost_estimate=cost(1, 1),
        name="begin",
    )(*caches, *owns, mine, other)


def finish_kernel(count, number, *refs):
    caches = refs[:count]
    query_all, top_ref, total_ref, numerator_ref, out_ref, scores = refs[count:]
    lines = query_all.shape[0] // 2
    some = slice(number * lines, (number + 1) * lines)
    top, total, numerator = weigh(
        query_all[some, :], caches, scores, top_ref[some, 0:1], total_ref[some, :], numerator_ref[some, :]
    )
    lane = lax.broadcasted_iota(jnp.int32, total.shape, 1)
    out_ref[:, :DH] = numerator
    out_ref[:, DH:] = jnp.where(lane < 64, top, jnp.sum(total, axis=1, keepdims=True))


def finish(caches, state, number):
    count = len(caches)
    lines = state[0].shape[0] // 2
    positions = count * caches[0].shape[1]
    return pl.pallas_call(
        functools.partial(finish_kernel, count, number),
        out_shape=jax.ShapeDtypeStruct((lines, DH + 128), jnp.float32),
        in_specs=in_vmem(count + 4),
        out_specs=in_vmem(1)[0],
        scratch_shapes=[pltpu.VMEM((lines, positions), jnp.float32)],
        compiler_params=params(24),
        cost_estimate=cost(8 * lines * positions * DH, 8 * lines * positions),
        name="finish",
    )(*caches, *state)


def output_term(attention, weights):
    return sum(
        jnp.dot(part, weight, preferred_element_type=jnp.float32) for part, weight in zip(attention, weights)
    )


def merge_kernel(rows, *refs):
    states, far_states = refs[:2], refs[2:4]
    mine, other, attention_ref = refs[4:7]
    outs = refs[7:]
    heads = states[0].shape[0] // rows
    parts = []
    for number in range(2):
        state, far_state = states[number], far_states[1 - number]
        top, far_top = state[:, DH : DH + 1], far_state[:, DH : DH + 1]
        peak = jnp.maximum(top, far_top)
        scale, far_scale = jnp.exp(top - peak), jnp.exp(far_top - peak)
        denominator = state[:, DH + 64 : DH + 65] * scale + far_state[:, DH + 64 : DH + 65] * far_scale
        numerator = state[:, :DH] * scale + far_state[:, :DH] * far_scale
        result = (numerator * (1.0 / denominator)).astype(jnp.bfloat16)
        for head in range(heads):
            attention_ref[number, :, head * DH : (head + 1) * DH] = result[head * rows : (head + 1) * rows, :]
        parts.append(attention_ref[number])
    for number, out in enumerate(outs):
        out[...] = output_term(parts, (mine[number], other[number])).astype(out.dtype)


def merge(states, far_states, mine, other, rows):
    count, depth, width = mine.shape
    return pl.pallas_call(
        functools.partial(merge_kernel, rows),
        out_shape=[jax.ShapeDtypeStruct((2, rows, depth), jnp.bfloat16)]
        + [jax.ShapeDtypeStruct((rows, width), jnp.bfloat16)] * count,
        in_specs=in_vmem(6),
        out_specs=in_vmem(1 + count),
        compiler_params=params(16),
        name="merge",
    )(*states, *far_states, mine, other)


def rest_kernel(attention, mine, other, *outs):
    for number, out in enumerate(outs):
        out[...] = output_term((attention[0], attention[1]), (mine[number], other[number]))


def rest(attention, mine, other):
    count, _, width = mine.shape
    return pl.pallas_call(
        rest_kernel,
        out_shape=[jax.ShapeDtypeStruct((attention.shape[1], width), jnp.float32)] * count,
        in_specs=in_vmem(3),
        out_specs=in_vmem(count),
        compiler_params=params(12),
        name="rest",
    )(attention, mine, other)


def body(tokens, gain, w_query, w_key, w_value, w_out, prefix_cache, size):
    chips = size // 2
    outer = chips // 2
    cycle = [2 * a for a in range(outer)] + [2 * a + 1 for a in reversed(range(outer))]

    def around(value, step):
        pairs = [
            (2 * cycle[p] + k, 2 * cycle[(p + step) % chips] + k) for p in range(chips) for k in (0, 1)
        ]
        return lax.ppermute(value, "seq", pairs)

    def swap(value, bits):
        return lax.ppermute(value, "seq", [(i, i ^ bits) for i in range(size)])

    rows = tokens.shape[0]

    block = pack(tokens, gain)
    blocks, offsets = [], []

    def take(value, offset):
        blocks.extend([value, swap(value, 1)])
        offsets.extend([(offset, False), (offset, True)])

    right = left = block
    reach = chips // 2
    take(block, 0)
    middle = w_query.shape[0] // 2
    weights = []
    first = tuple([reach] + ([chips - reach + 1] if reach > 1 else []))
    others = tuple(offset for offset in range(chips) if offset not in first)
    for step in range(1, reach + 1):
        if step > 1:
            right, weights = lax.optimization_barrier((right, weights))
        if step <= 2:
            w_query, right = lax.optimization_barrier((w_query, right))
            weights = [*weights, fetch(w_query, (step - 1) * middle, middle)]
        right = around(right, 1)
        if step == 1:
            prefix_cache, right = lax.optimization_barrier((prefix_cache, right))
            pieces = cut(prefix_cache, chips)
        if step == min(2, reach):
            pieces, right = lax.optimization_barrier((pieces, right))
        if step == max(reach - 1, 1):
            pieces, right = lax.optimization_barrier((pieces, right))
        take(right, -step)
        if step < reach:
            left = around(left, -1)
            take(left, step)

    soon = (chips - reach) // 2
    sooner = [*range(reach, reach + soon), *reversed(range(1, reach))]
    later = [*reversed(range(reach + soon, chips))]
    close = [swap(pieces[step], 2 * step) for step in sooner]
    pieces, close = lax.optimization_barrier((pieces, close))
    far_parts = [swap(pieces[step], 2 * step) for step in later]
    query, own = project(tuple(offsets), chips, blocks, *weights, w_key, w_value, rows)

    w_out, query = lax.optimization_barrier((w_out, query))
    sends = half(w_out, chips, (False, first), (False, others))
    query, own, sends = lax.optimization_barrier((query, own, sends))

    sharers = size // KV
    other_query = swap(query, 1)
    if sharers == 2:
        owns = [own, swap(own, 1)]
    else:
        groups = [list(range(g * sharers, (g + 1) * sharers)) for g in range(KV)]
        gathered = lax.all_gather(own, "seq", axis=0, axis_index_groups=groups)
        owns = [gathered[i] for i in range(sharers)]

    send_first, send_others = sends
    other_first = swap(send_first, 1)
    send_others, owns, other_query, close = lax.optimization_barrier((send_others, owns, other_query, close))
    other_others = swap(send_others, 1)
    state = begin([pieces[0], *close], owns, query, other_query)
    w_out, state = lax.optimization_barrier((w_out, state))
    mine_first, mine_others = half(w_out, chips, (True, first), (True, others))
    state, mine_first, mine_others = lax.optimization_barrier((state, mine_first, mine_others))
    ends = [finish(far_parts, state, number) for number in range(2)]
    swapped = [swap(end, 1) for end in ends]

    attention, *terms = merge(ends, swapped, mine_first, other_first, rows)
    terms = dict(zip(first, terms))
    terms.update(zip(others, rest(attention, mine_others, other_others)))
    right = left = None
    for step in reversed(range(1, reach + 1)):
        term = terms[step]
        right = term if right is None else (right.astype(jnp.float32) + term).astype(jnp.bfloat16)
        right = around(right, 1)
        if step < reach:
            term = terms[chips - step]
            left = term if left is None else (left.astype(jnp.float32) + term).astype(jnp.bfloat16)
            left = around(left, -1)
    total = terms[0] + right.astype(jnp.float32)
    if left is not None:
        total += left.astype(jnp.float32)
    return total.astype(jnp.bfloat16)


def solution(mesh):
    return jax.shard_map(
        functools.partial(body, size=mesh.shape["seq"]),
        mesh=mesh,
        in_specs=(
            P("group", "seq"),
            P("seq"),
            P("seq", None),
            P("seq", None),
            P("seq", None),
            P("seq", None),
            P(None, ("group", "seq"), None),
        ),
        out_specs=P("group", "seq"),
        check_vma=False,
    )
```

```python
import functools
import math

import jax
import jax.numpy as jnp
from jax import lax
from jax.experimental import pallas as pl
from jax.experimental.pallas import tpu as pltpu
from jax.sharding import PartitionSpec as P

H = 64
KV = 8
DH = 128
EPS = 1e-05
PAD = 16
MIB = 1 << 20
TRANS_B = (((1,), (1,)), ((), ()))


def in_vmem(count):
    return [pl.BlockSpec(memory_space=pltpu.VMEM)] * count


def anywhere(count):
    return [pl.BlockSpec(memory_space=pl.ANY)] * count


def cost(flops, moved):
    return pl.CostEstimate(flops=flops, bytes_accessed=moved, transcendentals=0)


def params(mib):
    return pltpu.CompilerParams(vmem_limit_bytes=mib * MIB)


def chip_at(place, chips):
    return jnp.where(place < chips // 2, 2 * place, 2 * (chips - 1 - place) + 1)


def place_of(chip, chips):
    return jnp.where(lax.rem(chip, 2) == 0, lax.div(chip, 2), chips - 1 - lax.div(chip, 2))


def here():
    device = lax.axis_index("seq")
    return lax.div(device, 2), lax.rem(device, 2)


def neighbour_chip(offset, chips):
    chip, _ = here()
    return chip_at(lax.rem(place_of(chip, chips) + offset + chips, chips), chips)


def pack_kernel(tokens, gain, block, near, sems):
    rows, width = tokens.shape
    copies = [
        pltpu.make_async_copy(gain, near, sems.at[0]),
        pltpu.make_async_copy(tokens, block.at[pl.ds(0, rows), :], sems.at[1]),
    ]
    for copy in copies:
        copy.start()
    copies[0].wait()
    wide = near[...].astype(jnp.float32).reshape(1, width)
    block[rows:, :] = jnp.broadcast_to(wide, (PAD, width)).astype(jnp.bfloat16)
    copies[1].wait()


def pack(tokens, gain):
    rows, width = tokens.shape
    return pl.pallas_call(
        pack_kernel,
        out_shape=pltpu.VMEM((rows + PAD, width), jnp.bfloat16),
        in_specs=anywhere(2),
        out_specs=in_vmem(1)[0],
        scratch_shapes=[pltpu.VMEM((width,), jnp.bfloat16), pltpu.SemaphoreType.DMA((2,))],
        name="pack",
    )(in_hbm(tokens), in_hbm(gain))


def cut_kernel(chips, cache, *pieces):
    chip, _ = here()
    for step, piece in enumerate(pieces):
        head = lax.div(lax.bitwise_xor(chip, step) * KV, chips)
        piece[...] = cache[:, :, pl.ds(pl.multiple_of(head * DH, DH), DH)]


def cut(cache, chips):
    shape = (2, cache.shape[1], DH)
    return pl.pallas_call(
        functools.partial(cut_kernel, chips),
        out_shape=[jax.ShapeDtypeStruct(shape, jnp.bfloat16)] * chips,
        in_specs=in_vmem(1),
        out_specs=in_vmem(chips),
        compiler_params=params(8),
        name="cut",
    )(cache)


def half_kernel(groups, chips, width, w_out, *refs):
    outs, sems = refs[:-1], refs[-1]
    _, core = here()
    copies = []
    for out, (mine, offsets) in zip(outs, groups):
        for number, offset in enumerate(offsets):
            column = 2 * neighbour_chip(offset, chips) + (core if mine else 1 - core)
            columns = pl.ds(pl.multiple_of(column * width, width), width)
            copy = pltpu.make_async_copy(w_out.at[:, columns], out.at[number], sems.at[len(copies)])
            copy.start()
            copies.append(copy)
    for copy in copies:
        copy.wait()


def in_hbm(value):
    return pltpu.with_memory_space_constraint(value, pltpu.HBM)


def half(w_out, chips, *groups):
    rows, columns = w_out.shape
    width = columns // (2 * chips)
    return pl.pallas_call(
        functools.partial(half_kernel, groups, chips, width),
        out_shape=[jax.ShapeDtypeStruct((len(offsets), rows, width), jnp.bfloat16) for _, offsets in groups],
        in_specs=anywhere(1),
        out_specs=in_vmem(len(groups)),
        scratch_shapes=[pltpu.SemaphoreType.DMA((sum(len(offsets) for _, offsets in groups),))],
        compiler_params=params(12),
        name="half",
    )(in_hbm(w_out))


def fetch_kernel(start, size, source, target, sem):
    copy = pltpu.make_async_copy(source.at[pl.ds(start, size), :], target, sem)
    copy.start()
    copy.wait()


def fetch(value, start, size):
    return pl.pallas_call(
        functools.partial(fetch_kernel, start, size),
        out_shape=pltpu.VMEM((size, value.shape[1]), jnp.bfloat16),
        in_specs=anywhere(1),
        out_specs=in_vmem(1)[0],
        scratch_shapes=[pltpu.SemaphoreType.DMA],
        compiler_params=params(8),
        cost_estimate=cost(0, 4 * size * value.shape[1]),
        name="fetch",
    )(in_hbm(value))


def project_kernel(offsets, chips, rows, *refs):
    count = len(offsets)
    blocks = refs[:count]
    w_first, w_second, w_key, w_value, query_ref, own_ref, held_own, own_sems = refs[count:]
    width = blocks[0].shape[1]
    side, middle = w_key.shape[0], w_first.shape[0]
    _, core = here()
    own_copies = [
        pltpu.make_async_copy(w_key, held_own.at[pl.ds(0, side), :], own_sems.at[0]),
        pltpu.make_async_copy(w_value, held_own.at[pl.ds(side, side), :], own_sems.at[1]),
    ]
    for copy in own_copies:
        copy.start()
    total = jnp.zeros((rows, 128), jnp.float32)
    for block in blocks:
        wide = block[:rows, :].astype(jnp.float32)
        square = wide * wide
        for lane in range(0, width, 128):
            total += square[:, lane : lane + 128]
    inverse = lax.rsqrt(jnp.sum(total, axis=1, keepdims=True) / (width * count) + EPS)
    first = jnp.zeros((rows, middle), jnp.float32)
    second = jnp.zeros((rows, middle), jnp.float32)
    own = jnp.zeros(own_ref.shape, jnp.float32)
    for copy in own_copies:
        copy.wait()
    for block, (offset, other) in zip(blocks, offsets):
        owner = 2 * neighbour_chip(offset, chips) + (1 - core if other else core)
        columns = pl.ds(pl.multiple_of(owner * width, width), width)
        gain = block[rows : rows + PAD, :].astype(jnp.float32)[0:1, :]
        wide = block[:rows, :].astype(jnp.float32)
        normed = (wide * inverse * gain).astype(jnp.bfloat16)
        own += lax.dot_general(normed, held_own[:, columns], TRANS_B, preferred_element_type=jnp.float32)
        first += lax.dot_general(normed, w_first[:, columns], TRANS_B, preferred_element_type=jnp.float32)
        second += lax.dot_general(normed, w_second[:, columns], TRANS_B, preferred_element_type=jnp.float32)
    query_ref[:, :middle] = first.astype(jnp.bfloat16)
    query_ref[:, middle:] = second.astype(jnp.bfloat16)
    own_ref[...] = own.astype(jnp.bfloat16)


def project(offsets, chips, blocks, w_first, w_second, w_key, w_value, rows):
    count = len(blocks)
    return pl.pallas_call(
        functools.partial(project_kernel, offsets, chips, rows),
        out_shape=(
            jax.ShapeDtypeStruct((rows, 2 * w_first.shape[0]), jnp.bfloat16),
            jax.ShapeDtypeStruct((rows, 2 * w_key.shape[0]), jnp.bfloat16),
        ),
        in_specs=in_vmem(count + 2) + anywhere(2),
        out_specs=tuple(in_vmem(2)),
        scratch_shapes=[
            pltpu.VMEM((2 * w_key.shape[0], w_key.shape[1]), jnp.bfloat16),
            pltpu.SemaphoreType.DMA((2,)),
        ],
        compiler_params=params(12),
        name="project",
    )(*blocks, w_first, w_second, in_hbm(w_key), in_hbm(w_value))


def weigh(query, caches, scores, top, total, numerator):
    scale = 1.0 / math.sqrt(DH)
    step = caches[0].shape[1]
    best = None
    for number, cache in enumerate(caches):
        part = lax.dot_general(query, cache[0], TRANS_B, preferred_element_type=jnp.float32)
        scores[:, number * step : (number + 1) * step] = part
        for lane in range(0, step, 128):
            piece = part[:, lane : lane + 128]
            best = piece if best is None else jnp.maximum(best, piece)
    before = top
    top = jnp.maximum(jnp.max(best, axis=1, keepdims=True) * scale, top)
    shrink = jnp.exp(before - top)
    total, numerator = total * shrink, numerator * shrink
    for number, cache in enumerate(caches):
        weights = jnp.exp(scores[:, number * step : (number + 1) * step] * scale - top)
        for lane in range(0, step, 128):
            total += weights[:, lane : lane + 128]
        numerator += jnp.dot(weights.astype(jnp.bfloat16), cache[1], preferred_element_type=jnp.float32)
    return top, total, numerator


def begin_kernel(count, parts, heads, *refs):
    caches, owns = refs[:count], refs[count : count + parts]
    mine, other, query_all, top_ref, total_ref, numerator_ref, scores = refs[count + parts :]
    rows = mine.shape[0]
    lines = heads * rows
    side = owns[0].shape[1] // 2
    _, core = here()
    own_parts = [own[...].astype(jnp.float32) for own in owns]
    if parts == 2:
        own_parts = [jnp.where(core == 0, own_parts[i], own_parts[1 - i]) for i in range(2)]
    own_key = jnp.concatenate([part[:, :side] for part in own_parts], axis=1)
    own_value = jnp.concatenate([part[:, side:] for part in own_parts], axis=1)
    for number, query_ref in enumerate((mine, other)):
        for head in range(heads):
            start = number * lines + head * rows
            query_all[start : start + rows, :] = query_ref[:, head * DH : (head + 1) * DH]
    lane = lax.broadcasted_iota(jnp.int32, (rows, 128), 1)
    for start in range(0, 2 * lines, rows):
        some = slice(start, start + rows)
        query = query_all[some, :]
        own = jnp.sum(query.astype(jnp.float32) * own_key, axis=1, keepdims=True) / math.sqrt(DH)
        mine_here = start < lines
        total = jnp.where(lane == 0, 1.0, 0.0) if mine_here else jnp.zeros((rows, 128), jnp.float32)
        numerator = own_value if mine_here else jnp.zeros((rows, DH), jnp.float32)
        top, total, numerator = weigh(query, caches, scores.at[some, :], own, total, numerator)
        top_ref[some, :] = jnp.broadcast_to(top, (rows, 128))
        total_ref[some, :] = total
        numerator_ref[some, :] = numerator


def begin(caches, owns, mine, other):
    count, rows = len(caches), mine.shape[0]
    heads = mine.shape[1] // DH
    lines = 2 * heads * rows
    positions = count * caches[0].shape[1]
    return pl.pallas_call(
        functools.partial(begin_kernel, count, len(owns), heads),
        out_shape=[jax.ShapeDtypeStruct((lines, DH), jnp.bfloat16)]
        + [jax.ShapeDtypeStruct((lines, 128), jnp.float32)] * 3,
        in_specs=in_vmem(count + len(owns) + 2),
        out_specs=in_vmem(4),
        scratch_shapes=[pltpu.VMEM((lines, positions), jnp.float32)],
        compiler_params=params(24),
        cost_estimate=cost(1, 1),
        name="begin",
    )(*caches, *owns, mine, other)


def finish_kernel(count, number, *refs):
    caches = refs[:count]
    query_all, top_ref, total_ref, numerator_ref, out_ref, scores = refs[count:]
    lines = query_all.shape[0] // 2
    some = slice(number * lines, (number + 1) * lines)
    top, total, numerator = weigh(
        query_all[some, :], caches, scores, top_ref[some, 0:1], total_ref[some, :], numerator_ref[some, :]
    )
    lane = lax.broadcasted_iota(jnp.int32, total.shape, 1)
    out_ref[:, :DH] = numerator
    out_ref[:, DH:] = jnp.where(lane < 64, top, jnp.sum(total, axis=1, keepdims=True))


def finish(caches, state, number):
    count = len(caches)
    lines = state[0].shape[0] // 2
    positions = count * caches[0].shape[1]
    return pl.pallas_call(
        functools.partial(finish_kernel, count, number),
        out_shape=jax.ShapeDtypeStruct((lines, DH + 128), jnp.float32),
        in_specs=in_vmem(count + 4),
        out_specs=in_vmem(1)[0],
        scratch_shapes=[pltpu.VMEM((lines, positions), jnp.float32)],
        compiler_params=params(24),
        cost_estimate=cost(8 * lines * positions * DH, 8 * lines * positions),
        name="finish",
    )(*caches, *state)


def output_term(attention, weights):
    return sum(
        jnp.dot(part, weight, preferred_element_type=jnp.float32) for part, weight in zip(attention, weights)
    )


def merge_kernel(rows, *refs):
    states, far_states = refs[:2], refs[2:4]
    mine, other, attention_ref = refs[4:7]
    outs = refs[7:]
    heads = states[0].shape[0] // rows
    parts = []
    for number in range(2):
        state, far_state = states[number], far_states[1 - number]
        top, far_top = state[:, DH : DH + 1], far_state[:, DH : DH + 1]
        peak = jnp.maximum(top, far_top)
        scale, far_scale = jnp.exp(top - peak), jnp.exp(far_top - peak)
        denominator = state[:, DH + 64 : DH + 65] * scale + far_state[:, DH + 64 : DH + 65] * far_scale
        numerator = state[:, :DH] * scale + far_state[:, :DH] * far_scale
        result = (numerator * (1.0 / denominator)).astype(jnp.bfloat16)
        for head in range(heads):
            attention_ref[number, :, head * DH : (head + 1) * DH] = result[head * rows : (head + 1) * rows, :]
        parts.append(attention_ref[number])
    for number, out in enumerate(outs):
        out[...] = output_term(parts, (mine[number], other[number])).astype(out.dtype)


def merge(states, far_states, mine, other, rows):
    count, depth, width = mine.shape
    return pl.pallas_call(
        functools.partial(merge_kernel, rows),
        out_shape=[jax.ShapeDtypeStruct((2, rows, depth), jnp.bfloat16)]
        + [jax.ShapeDtypeStruct((rows, width), jnp.bfloat16)] * count,
        in_specs=in_vmem(6),
        out_specs=in_vmem(1 + count),
        compiler_params=params(16),
        name="merge",
    )(*states, *far_states, mine, other)


def rest_kernel(attention, mine, other, *outs):
    for number, out in enumerate(outs):
        out[...] = output_term((attention[0], attention[1]), (mine[number], other[number]))


def rest(attention, mine, other):
    count, _, width = mine.shape
    return pl.pallas_call(
        rest_kernel,
        out_shape=[jax.ShapeDtypeStruct((attention.shape[1], width), jnp.float32)] * count,
        in_specs=in_vmem(3),
        out_specs=in_vmem(count),
        compiler_params=params(12),
        name="rest",
    )(attention, mine, other)


def body(tokens, gain, w_query, w_key, w_value, w_out, prefix_cache, size):
    chips = size // 2
    outer = chips // 2
    cycle = [2 * a for a in range(outer)] + [2 * a + 1 for a in reversed(range(outer))]

    def around(value, step):
        pairs = [
            (2 * cycle[p] + k, 2 * cycle[(p + step) % chips] + k) for p in range(chips) for k in (0, 1)
        ]
        return lax.ppermute(value, "seq", pairs)

    def swap(value, bits):
        return lax.ppermute(value, "seq", [(i, i ^ bits) for i in range(size)])

    rows = tokens.shape[0]

    block = pack(tokens, gain)
    blocks, offsets = [], []

    def take(value, offset):
        blocks.extend([value, swap(value, 1)])
        offsets.extend([(offset, False), (offset, True)])

    right = left = block
    reach = chips // 2
    take(block, 0)
    middle = w_query.shape[0] // 2
    weights = []
    first = tuple([reach] + ([chips - reach + 1] if reach > 1 else []))
    others = tuple(offset for offset in range(chips) if offset not in first)
    for step in range(1, reach + 1):
        if step > 1:
            right, weights = lax.optimization_barrier((right, weights))
        if step <= 2:
            w_query, right = lax.optimization_barrier((w_query, right))
            weights = [*weights, fetch(w_query, (step - 1) * middle, middle)]
        right = around(right, 1)
        if step == 1:
            prefix_cache, right = lax.optimization_barrier((prefix_cache, right))
            pieces = cut(prefix_cache, chips)
        if step == min(2, reach):
            pieces, right = lax.optimization_barrier((pieces, right))
        if step == max(reach - 1, 1):
            pieces, right = lax.optimization_barrier((pieces, right))
        take(right, -step)
        if step < reach:
            left = around(left, -1)
            take(left, step)

    soon = (chips - reach) // 2
    sooner = [*range(reach, reach + soon), *reversed(range(1, reach))]
    later = [*reversed(range(reach + soon, chips))]
    close = [swap(pieces[step], 2 * step) for step in sooner]
    pieces, close = lax.optimization_barrier((pieces, close))
    far_parts = [swap(pieces[step], 2 * step) for step in later]
    query, own = project(tuple(offsets), chips, blocks, *weights, w_key, w_value, rows)

    w_out, query = lax.optimization_barrier((w_out, query))
    sends = half(w_out, chips, (False, first), (False, others))
    query, own, sends = lax.optimization_barrier((query, own, sends))

    sharers = size // KV
    other_query = swap(query, 1)
    if sharers == 2:
        owns = [own, swap(own, 1)]
    else:
        groups = [list(range(g * sharers, (g + 1) * sharers)) for g in range(KV)]
        gathered = lax.all_gather(own, "seq", axis=0, axis_index_groups=groups)
        owns = [gathered[i] for i in range(sharers)]

    send_first, send_others = sends
    other_first = swap(send_first, 1)
    send_others, owns, other_query, close[:-1] = lax.optimization_barrier(
        (send_others, owns, other_query, close[:-1])
    )
    other_others = swap(send_others, 1)
    state = begin([pieces[0], *close], owns, query, other_query)
    w_out, state = lax.optimization_barrier((w_out, state))
    mine_first, mine_others = half(w_out, chips, (True, first), (True, others))
    state, mine_first, mine_others = lax.optimization_barrier((state, mine_first, mine_others))
    ends = [finish(far_parts, state, number) for number in range(2)]
    swapped = [swap(end, 1) for end in ends]

    attention, *terms = merge(ends, swapped, mine_first, other_first, rows)
    terms = dict(zip(first, terms))
    terms.update(zip(others, rest(attention, mine_others, other_others)))
    right = left = None
    for step in reversed(range(1, reach + 1)):
        term = terms[step]
        right = term if right is None else (right.astype(jnp.float32) + term).astype(jnp.bfloat16)
        right = around(right, 1)
        if step < reach:
            term = terms[chips - step]
            left = term if left is None else (left.astype(jnp.float32) + term).astype(jnp.bfloat16)
            left = around(left, -1)
    total = terms[0] + right.astype(jnp.float32)
    if left is not None:
        total += left.astype(jnp.float32)
    return total.astype(jnp.bfloat16)


def solution(mesh):
    return jax.shard_map(
        functools.partial(body, size=mesh.shape["seq"]),
        mesh=mesh,
        in_specs=(
            P("group", "seq"),
            P("seq"),
            P("seq", None),
            P("seq", None),
            P("seq", None),
            P("seq", None),
            P(None, ("group", "seq"), None),
        ),
        out_specs=P("group", "seq"),
        check_vma=False,
    )
```
